256 devices in a mesh: lon: 16 (over z, y_lo), lat: 16 (over y_hi, x, core).
Axes of the slice: x: 4, y: 4 (y_hi: 2, y_lo: 2; y = y_hi * 2 + y_lo), z: 8, core: 2. Of those that a mesh axis runs over, the one named last changes fastest.
Arguments:
- tokens: bfloat16 [256, 1024, 128], P('lat', 'lon'), may hold values from -40 to 40
- region1: int32 [256, 1024], P('lat', 'lon'), may hold values from 0 to 1
- region2: int32 [128, 512], P('lat', 'lon'), may hold values from 0 to 1
- bias_index: int32 [64, 64], replicated, may hold values from 0 to 224
- ln1_gain: float32 [128], replicated, may hold values from 0.1 to 1.9
- qkv_weight1: bfloat16 [128, 384], replicated, may hold values from -2.5 to 2.5
- out_weight1: bfloat16 [128, 128], replicated, may hold values from -0.5 to 0.5
- bias_table1: float32 [225, 4], replicated, may hold values from -4 to 4
- merge_gain: float32 [512], replicated, may hold values from 0.1 to 1.9
- merge_weight: bfloat16 [512, 256], replicated, may hold values from -0.25 to 0.25
- ln2_gain: float32 [256], replicated, may hold values from 0.1 to 1.9
- qkv_weight2: bfloat16 [256, 768], replicated, may hold values from -2.5 to 2.5
- out_weight2: bfloat16 [256, 256], replicated, may hold values from -0.375 to 0.375
- bias_table2: float32 [225, 8], replicated, may hold values from -4 to 4
- cot_fine: bfloat16 [256, 1024, 128], P('lat', 'lon'), may hold values from -6 to 6
- cot_coarse: bfloat16 [128, 512, 256], P('lat', 'lon'), may hold values from -6 to 6
Outputs:
- coarse_out: bfloat16 [128, 512, 256], P('lat', 'lon')
- grad_tokens: bfloat16 [256, 1024, 128], P('lat', 'lon')
- grad_ln1_gain: float32 [128], replicated
- grad_qkv1: float32 [128, 384], replicated
- grad_out1: float32 [128, 128], replicated
- grad_table1: float32 [225, 4], replicated
- grad_merge_gain: float32 [512], replicated
- grad_merge: float32 [512, 256], replicated
- grad_ln2_gain: float32 [256], replicated
- grad_qkv2: float32 [256, 768], replicated
- grad_out2: float32 [256, 256], replicated
- grad_table2: float32 [225, 8], replicated
The draws below stay inside these ranges and needn't reach their ends.
All inputs are finite; a program needn't handle non-finite values.
Results may differ from the reference program's by a relative error of at most 0.029.
The reference program's roundings to bfloat16 on the way count: a program that leaves them out, or rounds other values in their place, can miss the bound.
Values may be sent and summed in bfloat16 or wider, within the bound.
No kernel may reach another device: no remote copies, remote signals or barrier semaphores. Data moves between devices by JAX's collectives and lax.ppermute only.
A program may use at most 64 MiB of HBM per device.

```python
import math
from functools import partial
import jax
import jax.numpy as jnp
from jax import lax

C = 128
WIN = 8
HEADS1 = 4
C2 = 256
HEADS2 = 8
TABLE = 225
NL = 256
NW = 1024


def drawn_weight(key, model_width):
    base_key = jax.random.fold_in(key, 0)
    base_part = jax.random.normal(base_key, (model_width, 3 * model_width), jnp.float32) * model_width ** (-0.5)
    query_part = base_part[:, :model_width]
    key_part = base_part[:, model_width:2 * model_width]
    joined = jnp.concatenate((query_part, key_part, base_part[:, 2 * model_width:]), axis=1)
    return jnp.clip(joined, -2.5, 2.5).astype(jnp.bfloat16)


def draw_tokens(key, part):
    key = jax.random.fold_in(key, 7)
    noise_key, row_key, col_key = jax.random.split(key, 3)
    noise_part = jnp.clip(jax.random.normal(noise_key, (NL, NW, C), jnp.float32), -4.0, 4.0)
    row_range = math.log(10.0)
    row_scale = jnp.exp(jax.random.uniform(row_key, (NL, NW, 1), jnp.float32, 0.0, row_range))
    col_scale = jnp.exp(jax.random.uniform(col_key, (C,), jnp.float32, 0.0, math.log(10.0)))
    return (noise_part * row_scale * col_scale * 0.1).astype(jnp.bfloat16)


def draw_qkv_weight1(key, part):
    key = jax.random.fold_in(key, 11)
    return drawn_weight(key, C)


def draw_qkv_weight2(key, part):
    key = jax.random.fold_in(key, 13)
    return drawn_weight(key, C2)


def plant(entries, rng, least, top_value):
    longest = entries.shape.index(max(entries.shape))
    spots = []
    for shift in (0, 1):
        where = [jax.random.randint(jax.random.fold_in(rng, axis), (), 0, length) for axis, length in enumerate(entries.shape)]
        where[longest] = (where[longest] + shift) % entries.shape[longest]
        spots.append(tuple(where))
    return entries.at[spots[0]].set(least).at[spots[1]].set(top_value)


def level_of(own_key, dims, shards, low, top_value):
    def one(dim, blocks):
        steps = jax.random.uniform(jax.random.fold_in(jax.random.fold_in(own_key, 6), dim), (blocks,), jnp.float32, low / len(shards), top_value / len(shards))
        return jnp.repeat(jnp.exp(steps), dims[dim] // blocks).reshape((-1,) + (1,) * (len(dims) - dim - 1))

    level = one(*shards[0])
    for cut in shards[1:]:
        level = level * one(*cut)
    return level


def scatter_about(own_key, dims, deviation, bound, shards=(), kind=jnp.bfloat16):
    entries = deviation * jax.random.normal(own_key, dims, jnp.float32)
    if shards:
        entries = entries * level_of(own_key, dims, shards, -0.22, 0.18)
    return jnp.clip(entries, -bound, bound).astype(kind)


def setup_inputs(seed: int = 0) -> dict:
    keys = jax.random.split(jax.random.key(seed), 17)
    return {
        "tokens": draw_tokens(jax.random.fold_in(keys[16], 71), 0),
        "region1": plant(jax.random.randint(keys[1], (NL, NW), 0, 2), jax.random.fold_in(keys[1], 1), 0, 1).astype(jnp.int32),
        "region2": plant(jax.random.randint(keys[2], (NL // 2, NW // 2), 0, 2), jax.random.fold_in(keys[2], 1), 0, 1).astype(jnp.int32),
        "bias_index": plant(jax.random.randint(keys[3], (WIN * WIN, WIN * WIN), 0, TABLE), jax.random.fold_in(keys[3], 1), 0, TABLE - 1).astype(jnp.int32),
        "ln1_gain": jnp.clip(1.0 + 0.18 * jax.random.normal(keys[4], (C,), jnp.float32), 0.1, 1.9),
        "qkv_weight1": draw_qkv_weight1(jax.random.fold_in(keys[16], 71), 0),
        "out_weight1": scatter_about(keys[6], (C, C), C ** -0.5, 0.5),
        "bias_table1": scatter_about(keys[7], (TABLE, HEADS1), 1.0, 4.0, (), jnp.float32),
        "merge_gain": jnp.clip(1.0 + 0.18 * jax.random.normal(keys[8], (4 * C,), jnp.float32), 0.1, 1.9),
        "merge_weight": scatter_about(keys[9], (4 * C, C2), (4 * C) ** -0.5, 0.25),
        "ln2_gain": jnp.clip(1.0 + 0.18 * jax.random.normal(keys[10], (C2,), jnp.float32), 0.1, 1.9),
        "qkv_weight2": draw_qkv_weight2(jax.random.fold_in(keys[16], 71), 0),
        "out_weight2": scatter_about(keys[12], (C2, C2), C2 ** -0.5, 0.375),
        "bias_table2": scatter_about(keys[13], (TABLE, HEADS2), 1.0, 4.0, (), jnp.float32),
        "cot_fine": scatter_about(keys[14], (NL, NW, C), 1.0, 6.0, ((0, 16), (1, 16))),
        "cot_coarse": scatter_about(keys[15], (NL // 2, NW // 2, C2), 1.0, 6.0, ((0, 16), (1, 16))),
    }


EPSILON = 1e-05
MASKED = -1000000000.0

def normed(inputs, norm_gain):
    row_mean = lax.optimization_barrier(jnp.mean(inputs, axis=-1, keepdims=True))
    centered = inputs - row_mean
    spread = lax.optimization_barrier(jnp.mean(centered * centered, axis=-1, keepdims=True))
    return (centered * lax.rsqrt(spread + EPSILON) * norm_gain).astype(jnp.bfloat16)

def to_windows(field_in, window_side):
    row_count, col_count, feature_count = field_in.shape
    shaped = field_in.reshape(row_count // window_side, window_side, col_count // window_side, window_side, feature_count)
    return shaped.transpose(0, 2, 1, 3, 4).reshape(-1, window_side * window_side, feature_count)

def from_windows(blocks, row_count, col_count, window_side):
    feature_count = blocks.shape[-1]
    shaped = blocks.reshape(row_count // window_side, col_count // window_side, window_side, window_side, feature_count)
    return shaped.transpose(0, 2, 1, 3, 4).reshape(row_count, col_count, feature_count)

def attend(qkv_blocks, bias_table, allowed, bias_index, head_count):
    window_count, token_count, triple_width = qkv_blocks.shape
    model_width = triple_width // 3
    head_size = model_width // head_count
    wide_blocks = qkv_blocks.astype(jnp.float32)
    query_part = wide_blocks[..., :model_width].reshape(window_count, token_count, head_count, head_size)
    key_part = wide_blocks[..., model_width:2 * model_width].reshape(window_count, token_count, head_count, head_size)
    value_part = wide_blocks[..., 2 * model_width:].reshape(window_count, token_count, head_count, head_size)
    scores = jnp.einsum('wihd,wjhd->whij', query_part, key_part) * head_size ** (-0.5)
    bias_heads = jnp.transpose(bias_table[bias_index], (2, 0, 1))
    scores = jnp.where(allowed[:, None], scores + bias_heads[None], MASKED)
    row_max = lax.optimization_barrier(jnp.max(scores, axis=-1, keepdims=True))
    exp_scores = jnp.exp(scores - row_max)
    weights = (exp_scores / lax.optimization_barrier(jnp.sum(exp_scores, axis=-1, keepdims=True))).astype(jnp.bfloat16)
    mixed_heads = jnp.einsum('whij,wjhd->wihd', weights.astype(jnp.float32), value_part)
    return mixed_heads.astype(jnp.bfloat16).reshape(window_count, token_count, model_width)

def layer_forward(region_in, key_field, norm_gain, w_qkv, w_out, bias_table, bias_index, head_count):
    row_count, col_count, model_width = region_in.shape
    wide_input = region_in.astype(jnp.float32)
    unit_normed, norm_pull = jax.vjp(normed, wide_input, norm_gain)
    qkv_flat = jnp.dot(unit_normed.reshape(-1, model_width), w_qkv, preferred_element_type=jnp.float32).astype(jnp.bfloat16)
    qkv_blocks = to_windows(qkv_flat.reshape(row_count, col_count, 3 * model_width), WIN)
    window_keys = to_windows(key_field[..., None], WIN)[..., 0]
    allowed = window_keys[:, :, None] == window_keys[:, None, :]
    attend_part = partial(attend, allowed=allowed, bias_index=bias_index, head_count=head_count)
    mixed_blocks, attend_pull = jax.vjp(attend_part, qkv_blocks, bias_table)
    flat_mixed = from_windows(mixed_blocks, row_count, col_count, WIN).reshape(-1, model_width)
    projected = jnp.dot(flat_mixed, w_out, preferred_element_type=jnp.float32).reshape(row_count, col_count, model_width)
    result = (wide_input + projected).astype(jnp.bfloat16)
    return (result, (unit_normed, flat_mixed, norm_pull, attend_pull))

def layer_backward(cotangent, saved_state, w_qkv, w_out):
    unit_normed, flat_mixed, norm_pull, attend_pull = saved_state
    row_count, col_count, model_width = cotangent.shape
    cot_flat = cotangent.reshape(-1, model_width)
    grad_out = jnp.dot(flat_mixed.T, cot_flat, preferred_element_type=jnp.float32)
    cot_mixed = jnp.dot(cot_flat, w_out.T, preferred_element_type=jnp.float32).astype(jnp.bfloat16)
    cot_blocks, grad_table = attend_pull(to_windows(cot_mixed.reshape(row_count, col_count, model_width), WIN))
    cot_qkv = from_windows(cot_blocks, row_count, col_count, WIN).reshape(-1, 3 * model_width)
    grad_qkv = jnp.dot(unit_normed.reshape(-1, model_width).T, cot_qkv, preferred_element_type=jnp.float32)
    cot_unit = jnp.dot(cot_qkv, w_qkv.T, preferred_element_type=jnp.float32).astype(jnp.bfloat16).reshape(row_count, col_count, model_width)
    cot_wide, grad_gain = norm_pull(cot_unit)
    cot_input = (cotangent.astype(jnp.float32) + cot_wide).astype(jnp.bfloat16)
    return (cot_input, (grad_gain, grad_qkv, grad_out, grad_table))

def side_keys(region_labels):
    row_count = region_labels.shape[0]
    row_ids = jnp.arange(row_count, dtype=jnp.int32)
    wrapped = (row_ids >= row_count - WIN // 2).astype(jnp.int32)
    return region_labels * 2 + wrapped[:, None]

def pack_quads(field_in):
    row_count, col_count, feature_count = field_in.shape
    shaped = field_in.reshape(row_count // 2, 2, col_count // 2, 2, feature_count)
    return shaped.transpose(0, 2, 3, 1, 4).reshape(row_count // 2, col_count // 2, 4 * feature_count)

def unpack_quads(field_in):
    row_count, col_count, feature_count = field_in.shape
    shaped = field_in.reshape(row_count, col_count, 2, 2, feature_count // 4)
    return shaped.transpose(0, 3, 1, 2, 4).reshape(2 * row_count, 2 * col_count, feature_count // 4)

def forward_bands(shifted_field, key_field, norm_gain, w_qkv, w_out, bias_table, bias_index, head_count):
    row_count, col_count, model_width = shifted_field.shape
    bands = shifted_field.reshape(row_count // WIN, WIN, col_count, model_width)
    key_bands = key_field.reshape(row_count // WIN, WIN, col_count)

    def one_band(items):
        return layer_forward(items[0], items[1], norm_gain, w_qkv, w_out, bias_table, bias_index, head_count)[0]
    return lax.map(one_band, (bands, key_bands)).reshape(row_count, col_count, model_width)

def backward_bands(shifted_field, key_field, cot_field, norm_gain, w_qkv, w_out, bias_table, bias_index, head_count):
    row_count, col_count, model_width = shifted_field.shape
    bands = shifted_field.reshape(row_count // WIN, WIN, col_count, model_width)
    key_bands = key_field.reshape(row_count // WIN, WIN, col_count)
    cot_bands = cot_field.reshape(row_count // WIN, WIN, col_count, model_width)

    def one_band(totals, items):
        _, saved_state = layer_forward(items[0], items[1], norm_gain, w_qkv, w_out, bias_table, bias_index, head_count)
        cot_input, grads = layer_backward(items[2], saved_state, w_qkv, w_out)
        return (jax.tree.map(jnp.add, totals, grads), cot_input)
    start = (jnp.zeros(norm_gain.shape, jnp.float32), jnp.zeros(w_qkv.shape, jnp.float32), jnp.zeros(w_out.shape, jnp.float32), jnp.zeros(bias_table.shape, jnp.float32))
    totals, cot_bands_in = lax.scan(one_band, start, (bands, key_bands, cot_bands))
    return (cot_bands_in.reshape(row_count, col_count, model_width), totals)

def reference(tokens, region1, region2, bias_index, ln1_gain, qkv_weight1, out_weight1, bias_table1, merge_gain, merge_weight, ln2_gain, qkv_weight2, out_weight2, bias_table2, cot_fine, cot_coarse):
    rim_width = WIN // 2

    def forth(field_in):
        return jnp.roll(field_in, (-rim_width, -rim_width), (0, 1))

    def restore(field_in):
        return jnp.roll(field_in, (rim_width, rim_width), (0, 1))
    keys_fine = side_keys(region1)
    keys_coarse = side_keys(region2)
    shifted = forth(tokens)
    fine_out = restore(forward_bands(shifted, keys_fine, ln1_gain, qkv_weight1, out_weight1, bias_table1, bias_index, HEADS1))
    joined = pack_quads(fine_out).astype(jnp.float32)
    merged_norm, merge_pull = jax.vjp(normed, joined, merge_gain)
    coarse_rows, coarse_cols = (joined.shape[0], joined.shape[1])
    coarse_in = jnp.dot(merged_norm.reshape(-1, 4 * C), merge_weight, preferred_element_type=jnp.float32).astype(jnp.bfloat16).reshape(coarse_rows, coarse_cols, C2)
    coarse_shift = forth(coarse_in)
    coarse_out = restore(forward_bands(coarse_shift, keys_coarse, ln2_gain, qkv_weight2, out_weight2, bias_table2, bias_index, HEADS2))
    cot_back2, grads2 = backward_bands(coarse_shift, keys_coarse, forth(cot_coarse), ln2_gain, qkv_weight2, out_weight2, bias_table2, bias_index, HEADS2)
    cot_coarse_in = restore(cot_back2)
    flat_cot = cot_coarse_in.reshape(-1, C2)
    grad_merge = jnp.dot(merged_norm.reshape(-1, 4 * C).T, flat_cot, preferred_element_type=jnp.float32)
    cot_norm = jnp.dot(flat_cot, merge_weight.T, preferred_element_type=jnp.float32).astype(jnp.bfloat16).reshape(merged_norm.shape)
    cot_joined, grad_merge_gain = merge_pull(cot_norm)
    cot_fine_out = (cot_fine.astype(jnp.float32) + unpack_quads(cot_joined)).astype(jnp.bfloat16)
    cot_back1, grads1 = backward_bands(shifted, keys_fine, forth(cot_fine_out), ln1_gain, qkv_weight1, out_weight1, bias_table1, bias_index, HEADS1)
    grad_tokens = restore(cot_back1)
    scale = 4.0 / math.sqrt(NL * NW)
    return (coarse_out, grad_tokens, grads1[0] * scale, grads1[1] * scale, grads1[2] * scale, grads1[3] * scale, grad_merge_gain * scale, grad_merge * scale, grads2[0] * scale, grads2[1] * scale, grads2[2] * scale, grads2[3] * scale)
```

```python
from functools import partial
import math

import jax
import jax.numpy as jnp
from jax import lax
from jax.experimental import pallas as pl
from jax.experimental.pallas import tpu as pltpu
from jax.sharding import PartitionSpec as P

WIN = 8
RIM = 4
TOK = WIN * WIN
EPSILON = 1e-05
MASKED = -1000000000.0
F32 = jnp.float32
BF16 = jnp.bfloat16
VMEM_LIMIT = 48 * 1024 * 1024


def nt_dot(a, b):
    return lax.dot_general(a, b, (((1,), (1,)), ((), ())), preferred_element_type=F32)


def tn_dot(a, b):
    return lax.dot_general(a, b, (((0,), (0,)), ((), ())), preferred_element_type=F32)


def nn_dot(a, b):
    return jnp.dot(a, b, preferred_element_type=F32)


def head_masks():
    rows = lax.broadcasted_iota(jnp.int32, (4 * TOK, 128), 0) // TOK
    lanes = lax.broadcasted_iota(jnp.int32, (4 * TOK, 128), 1) // 32
    return rows == lanes


def spread_heads(part, hm):
    return jnp.where(hm, jnp.concatenate([part] * 4, 0), jnp.zeros((), part.dtype))


def fold_heads(wide, hm):
    kept = jnp.where(hm, wide, 0.0)
    return (kept[:TOK] + kept[TOK : 2 * TOK]) + (kept[2 * TOK : 3 * TOK] + kept[3 * TOK :])


def probs(q4, k, bias, key_col, key_row):
    scores = nt_dot(k, q4) * (32 ** (-0.5)) + bias
    same = jnp.concatenate([key_col, key_col], 1) == key_row
    scores = jnp.where(same, scores, MASKED)
    top = jnp.max(scores, axis=0, keepdims=True)
    grown = jnp.exp(scores - top)
    return grown * (1.0 / jnp.sum(grown, axis=0, keepdims=True))


def unit_forward(q, k, v, bias, key_col, key_row, hm):
    weights = probs(spread_heads(q, hm), k, bias, key_col, key_row).astype(BF16)
    return fold_heads(tn_dot(weights, v), hm).astype(BF16)


def unit_backward(q, k, v, g, bias, key_col, key_row, hm):
    q4 = spread_heads(q, hm)
    g4 = spread_heads(g, hm)
    p = probs(q4, k, bias, key_col, key_row)
    dp = nt_dot(v, g4).astype(BF16).astype(F32)
    ds = p * (dp - jnp.sum(p * dp, axis=0, keepdims=True))
    dsb = (ds * (32 ** (-0.5))).astype(BF16)
    dq = fold_heads(tn_dot(dsb, k), hm).astype(BF16)
    dk = nn_dot(dsb, q4).astype(BF16)
    dv = nn_dot(p.astype(BF16), g4).astype(BF16)
    return dq, dk, dv, ds


def unit_norm(x):
    centered = x - jnp.mean(x, axis=-1, keepdims=True)
    rstd = lax.rsqrt(jnp.mean(centered * centered, axis=-1, keepdims=True) + EPSILON)
    return centered * rstd, rstd


def norm_back(hat, rstd, cot, gain):
    d = cot * gain
    return rstd * (
        d - jnp.mean(d, axis=-1, keepdims=True) - hat * jnp.mean(d * hat, axis=-1, keepdims=True)
    )


def pulled(field, own, rows, cols, corner, rim, rc, cc):
    feat = field.shape[-1]
    field[0:rc, 0:cc] = own.astype(F32)
    field[rc : rc + rim, 0:cc] = rows.astype(F32).reshape(rim, cc, feat)
    field[0:rc, cc : cc + rim] = cols.astype(F32).reshape(rc, rim, feat)
    field[rc : rc + rim, cc : cc + rim] = corner.astype(F32).reshape(rim, rim, feat)


def pushed(field, own, rows, cols, corner, rim, rc, cc):
    feat = field.shape[-1]
    field[rim : rim + rc, rim : rim + cc] = own.astype(F32)
    field[0:rim, rim : rim + cc] = rows.astype(F32).reshape(rim, cc, feat)
    field[rim : rim + rc, 0:rim] = cols.astype(F32).reshape(rc, rim, feat)
    field[0:rim, 0:rim] = corner.astype(F32).reshape(rim, rim, feat)


def fine_forward_kernel(
    x, xr, xc, xk, key_col, key_row, bias, gain, wqkv, wout,
    xw_out, qkv_out, mixed_out, own_out, row_out, col_out, corner_out,
    field, grid,
):
    rc, cc, feat = x.shape
    pulled(field, x[...], xr[...], xc[...], xk[...], RIM, rc, cc)
    hm = head_masks()
    wide = cc // WIN
    group = 4
    for a in range(rc // WIN):
        for b0 in range(0, wide, group):
            r0 = RIM + WIN * a
            parts = [
                field[r0 : r0 + WIN, RIM + WIN * b : RIM + WIN * (b + 1), :].reshape(TOK, feat)
                for b in range(b0, b0 + group)
            ]
            tokens = jnp.concatenate(parts, 0)
            t0 = (a * wide + b0) * TOK
            span = pl.ds(t0, group * TOK)
            xw_out[span, :] = tokens.astype(BF16)
            hat, _ = unit_norm(tokens)
            normed = (hat * gain[...]).astype(BF16)
            qkv = nn_dot(normed, wqkv[...]).astype(BF16)
            qkv_out[span, :] = qkv
            mixed = []
            for n in range(group):
                w = a * wide + b0 + n
                rows = slice(n * TOK, (n + 1) * TOK)
                mixed.append(
                    unit_forward(
                        qkv[rows, :feat],
                        qkv[rows, feat : 2 * feat],
                        qkv[rows, 2 * feat :],
                        bias[...],
                        key_col[w * TOK : (w + 1) * TOK, :],
                        key_row[w : w + 1, :],
                        hm,
                    )
                )
            mixed = jnp.concatenate(mixed, 0)
            mixed_out[span, :] = mixed
            result = tokens + nn_dot(mixed, wout[...])
            for n in range(group):
                b = b0 + n
                grid[WIN * a : WIN * (a + 1), WIN * b : WIN * (b + 1), :] = result[
                    n * TOK : (n + 1) * TOK
                ].reshape(WIN, WIN, feat)
    own_out[...] = grid[...].astype(BF16)
    row_out[...] = grid[0:RIM].reshape(RIM * cc, feat).astype(BF16)
    col_out[...] = grid[:, 0:RIM].reshape(rc * RIM, feat).astype(BF16)
    corner_out[...] = grid[0:RIM, 0:RIM].reshape(RIM * RIM, feat).astype(BF16)


def coarse_kernel(
    f, fr, fc, fk, cf, cfr, cfc, cfk, cc2, ccr, ccc, cck,
    key_col, key_row, bias, mgain, wmerge, gain, wqkv, wout,
    own_out, fine_out, row_out, col_out, corner_out,
    gmgain, gmerge, ggain, gqkv, gout, gbias,
    field, cfield, coarse_field, fgrid, cgrid,
):
    rc, cc, feat = f.shape
    r2, c2 = rc // 2, cc // 2
    feat2 = 2 * feat
    wide = c2 // WIN
    windows = [(a, b) for a in range(r2 // WIN) for b in range(wide)]
    count = len(windows) * TOK
    hm = head_masks()
    pulled(field, f[...], fr[...], fc[...], fk[...], RIM, rc, cc)
    pulled(cfield, cf[...], cfr[...], cfc[...], cfk[...], 2 * RIM, rc, cc)
    for half in range(2):
        lanes = slice(half * feat, (half + 1) * feat)
        pulled(
            coarse_field.at[half], cc2[:, :, lanes], ccr[half], ccc[half], cck[half], RIM, r2, c2
        )

    def in_windows(load):
        return jnp.concatenate([load(a, b).reshape(TOK, feat) for a, b in windows], 0)

    def joined_part(ref, rim, quad):
        dc, dr = quad // 2, quad % 2

        def load(a, b):
            return jnp.stack(
                [
                    ref[
                        rim + 2 * (WIN * a + r) + dr,
                        pl.ds(rim + 2 * WIN * b + dc, WIN, stride=2),
                        :,
                    ]
                    for r in range(WIN)
                ],
                0,
            )

        return in_windows(load)

    parts = [joined_part(field, RIM, quad) for quad in range(4)]
    mean = sum(jnp.sum(p, axis=-1, keepdims=True) for p in parts) * (1.0 / (4 * feat))
    centered = [p - mean for p in parts]
    spread = sum(jnp.sum(p * p, axis=-1, keepdims=True) for p in centered) * (1.0 / (4 * feat))
    mrstd = lax.rsqrt(spread + EPSILON)
    mhat = [p * mrstd for p in centered]
    mgains = [mgain[:, q * feat : (q + 1) * feat] for q in range(4)]
    mnormed = jnp.concatenate([(h * g).astype(BF16) for h, g in zip(mhat, mgains)], 1)
    coarse_in = nn_dot(mnormed, wmerge[...]).astype(BF16).astype(F32)
    hat, rstd = unit_norm(coarse_in)
    normed = (hat * gain[...]).astype(BF16)
    qkv = nn_dot(normed, wqkv[...]).astype(BF16)
    mixed = []
    for w in range(len(windows)):
        rows = slice(w * TOK, (w + 1) * TOK)
        units = []
        for g in range(2):
            lo = g * feat
            units.append(
                unit_forward(
                    qkv[rows, lo : lo + feat],
                    qkv[rows, feat2 + lo : feat2 + lo + feat],
                    qkv[rows, 2 * feat2 + lo : 2 * feat2 + lo + feat],
                    bias[:, g * 4 * TOK : (g + 1) * 4 * TOK],
                    key_col[rows, :],
                    key_row[w : w + 1, :],
                    hm,
                )
            )
        mixed.append(jnp.concatenate(units, 1))
    mixed = jnp.concatenate(mixed, 0)
    result = coarse_in + nn_dot(mixed, wout[...])
    for w, (a, b) in enumerate(windows):
        for half in range(2):
            cgrid[half, WIN * a : WIN * (a + 1), WIN * b : WIN * (b + 1), :] = result[
                w * TOK : (w + 1) * TOK, half * feat : (half + 1) * feat
            ].reshape(WIN, WIN, feat)
    cot = jnp.concatenate(
        [
            in_windows(
                lambda a, b: coarse_field[
                    half,
                    RIM + WIN * a : RIM + WIN * (a + 1),
                    RIM + WIN * b : RIM + WIN * (b + 1),
                    :,
                ]
            )
            for half in range(2)
        ],
        1,
    )
    cotb = cot.astype(BF16)
    gout[...] = tn_dot(mixed, cotb)
    cot_mixed = nt_dot(cotb, wout[...]).astype(BF16)
    cot_rows = []
    total = [jnp.zeros((TOK, 4 * TOK), F32) for _ in range(2)]
    for w in range(len(windows)):
        rows = slice(w * TOK, (w + 1) * TOK)
        dqs, dks, dvs = [], [], []
        for g in range(2):
            lo = g * feat
            dq, dk, dv, ds = unit_backward(
                qkv[rows, lo : lo + feat],
                qkv[rows, feat2 + lo : feat2 + lo + feat],
                qkv[rows, 2 * feat2 + lo : 2 * feat2 + lo + feat],
                cot_mixed[rows, lo : lo + feat],
                bias[:, g * 4 * TOK : (g + 1) * 4 * TOK],
                key_col[rows, :],
                key_row[w : w + 1, :],
                hm,
            )
            dqs.append(dq)
            dks.append(dk)
            dvs.append(dv)
            total[g] = total[g] + ds
        cot_rows.append(jnp.concatenate(dqs + dks + dvs, 1))
    gbias[...] = jnp.concatenate(total, 1)
    cot_qkv = jnp.concatenate(cot_rows, 0)
    gqkv[...] = tn_dot(normed, cot_qkv)
    cot_unit = nt_dot(cot_qkv, wqkv[...]).astype(BF16).astype(F32)
    ggain[...] = jnp.sum(cot_unit * hat, axis=0, keepdims=True)
    cot_in = (cot + norm_back(hat, rstd, cot_unit, gain[...])).astype(BF16)
    gmerge[...] = tn_dot(mnormed, cot_in)
    cot_norm = nt_dot(cot_in, wmerge[...]).astype(BF16).astype(F32)
    cot_parts = [cot_norm[:, q * feat : (q + 1) * feat] for q in range(4)]
    gmgain[...] = jnp.concatenate(
        [jnp.sum(c * h, axis=0, keepdims=True) for c, h in zip(cot_parts, mhat)], 1
    )
    ds = [c * g for c, g in zip(cot_parts, mgains)]
    mean_d = sum(jnp.sum(d, axis=-1, keepdims=True) for d in ds) * (1.0 / (4 * feat))
    mean_dh = sum(jnp.sum(d * h, axis=-1, keepdims=True) for d, h in zip(ds, mhat)) * (
        1.0 / (4 * feat)
    )
    for quad in range(4):
        dc, dr = quad // 2, quad % 2
        back = mrstd * (ds[quad] - mean_d - mhat[quad] * mean_dh)
        back = back + joined_part(cfield, 2 * RIM, quad)
        for w, (a, b) in enumerate(windows):
            for r in range(WIN):
                t0 = w * TOK + r * WIN
                fgrid[
                    2 * (WIN * a + r) + dr, pl.ds(2 * WIN * b + dc, WIN, stride=2), :
                ] = back[t0 : t0 + WIN]
    own_out[...] = jnp.concatenate([cgrid[0], cgrid[1]], -1).astype(BF16)
    fine_out[...] = fgrid[...].astype(BF16)
    nr, nc, nk = RIM * cc, rc * RIM, RIM * RIM
    row_out[0:nr] = fgrid[rc - RIM :].reshape(nr, feat).astype(BF16)
    col_out[0:nc] = fgrid[:, cc - RIM :].reshape(nc, feat).astype(BF16)
    corner_out[0:nk] = fgrid[rc - RIM :, cc - RIM :].reshape(nk, feat).astype(BF16)
    for half in range(2):
        row_out[nr + half * nr // 2 : nr + (half + 1) * nr // 2] = (
            cgrid[half, r2 - RIM :].reshape(nr // 2, feat).astype(BF16)
        )
        col_out[nc + half * nc // 2 : nc + (half + 1) * nc // 2] = (
            cgrid[half, :, c2 - RIM :].reshape(nc // 2, feat).astype(BF16)
        )
        corner_out[nk + half * nk : nk + (half + 1) * nk] = (
            cgrid[half, r2 - RIM :, c2 - RIM :].reshape(nk, feat).astype(BF16)
        )


def fine_backward_kernel(
    c, cr, cc_, ck, d, dr, dc, dk_, xw, qkv_in, mixed_in, key_col, key_row, bias, gain, wqkv, wout,
    own_out, row_out, col_out, corner_out, coarse_out, ggain, gqkv, gout, gbias,
    field, dfield, grid, cots,
):
    rc, cc, feat = c.shape
    r2, c2 = rc // 2, cc // 2
    pushed(field, c[...], cr[...], cc_[...], ck[...], RIM, rc, cc)
    for half in range(2):
        lanes = slice(half * feat, (half + 1) * feat)
        pushed(dfield.at[half], d[:, :, lanes], dr[half], dc[half], dk_[half], RIM, r2, c2)
        coarse_out[:, :, lanes] = dfield[half, 0:r2, 0:c2].astype(BF16)
    hm = head_masks()
    wide = cc // WIN
    group = 4
    total = jnp.zeros((TOK, 4 * TOK), F32)
    total_gain = jnp.zeros((1, feat), F32)
    total_out = jnp.zeros((feat, feat), F32)
    total_qkv = jnp.zeros((feat, 3 * feat), F32)
    for a in range(rc // WIN):
        for b0 in range(0, wide, group):
            cot = jnp.concatenate(
                [
                    field[
                        WIN * a : WIN * (a + 1), WIN * b : WIN * (b + 1), :
                    ].reshape(TOK, feat)
                    for b in range(b0, b0 + group)
                ],
                0,
            )
            t0 = (a * wide + b0) * TOK
            span = pl.ds(t0, group * TOK)
            cotb = cot.astype(BF16)
            total_out = total_out + tn_dot(mixed_in[span, :], cotb)
            cot_mixed = nt_dot(cotb, wout[...]).astype(BF16)
            qkv = qkv_in[span, :]
            cot_rows = []
            for n in range(group):
                w = a * wide + b0 + n
                rows = slice(n * TOK, (n + 1) * TOK)
                dq, dk, dv, ds = unit_backward(
                    qkv[rows, :feat],
                    qkv[rows, feat : 2 * feat],
                    qkv[rows, 2 * feat :],
                    cot_mixed[rows],
                    bias[...],
                    key_col[w * TOK : (w + 1) * TOK, :],
                    key_row[w : w + 1, :],
                    hm,
                )
                total = total + ds
                cot_rows.append(jnp.concatenate([dq, dk, dv], 1))
            cot_qkv = jnp.concatenate(cot_rows, 0)
            hat, rstd = unit_norm(xw[span, :].astype(F32))
            normed = (hat * gain[...]).astype(BF16)
            total_qkv = total_qkv + tn_dot(normed, cot_qkv)
            cot_unit = nt_dot(cot_qkv, wqkv[...]).astype(BF16).astype(F32)
            total_gain = total_gain + jnp.sum(cot_unit * hat, axis=0, keepdims=True)
            result = cot + norm_back(hat, rstd, cot_unit, gain[...])
            for n in range(group):
                b = b0 + n
                grid[WIN * a : WIN * (a + 1), WIN * b : WIN * (b + 1), :] = result[
                    n * TOK : (n + 1) * TOK
                ].reshape(WIN, WIN, feat)
    gbias[...] = total
    ggain[...] = total_gain
    gout[...] = total_out
    gqkv[...] = total_qkv
    own_out[...] = grid[...].astype(BF16)
    nr, nc, nk = RIM * cc, rc * RIM, RIM * RIM
    row_out[...] = grid[rc - RIM :].reshape(nr, feat).astype(BF16)
    col_out[...] = grid[:, cc - RIM :].reshape(nc, feat).astype(BF16)
    corner_out[...] = grid[rc - RIM :, cc - RIM :].reshape(nk, feat).astype(BF16)


def place_kernel(c, cr, cc_, ck, out, field):
    rc, cc, _ = c.shape
    pushed(field, c[...], cr[...], cc_[...], ck[...], RIM, rc, cc)
    out[...] = field[0:rc, 0:cc].astype(BF16)


def call(kernel, outs, scratch, *args):
    return pl.pallas_call(
        kernel,
        out_shape=outs,
        scratch_shapes=[pltpu.VMEM(s, F32) for s in scratch],
        compiler_params=pltpu.CompilerParams(vmem_limit_bytes=VMEM_LIMIT),
    )(*args)


def sds(*shape, dtype=BF16):
    return jax.ShapeDtypeStruct(shape, dtype)


def send(rows, cols, corner, sense):
    nlat, nlon = lax.axis_size("lat"), lax.axis_size("lon")
    lat = [(i, (i + sense) % nlat) for i in range(nlat)]
    lon = [(i, (i + sense) % nlon) for i in range(nlon)]
    both = [
        (j * nlat + i, (j + sense) % nlon * nlat + (i + sense) % nlat)
        for i in range(nlat)
        for j in range(nlon)
    ]
    return (
        lax.ppermute(rows, "lat", lat),
        lax.ppermute(cols, "lon", lon),
        lax.ppermute(corner, ("lon", "lat"), both),
    )


def halves(x):
    f = x.shape[-1] // 2
    x = x.reshape(-1, 2 * f)
    return jnp.concatenate([x[:, :f], x[:, f:]], 0)


def window_keys(labels):
    rows, cols = labels.shape
    first = lax.axis_index("lat") * rows
    last = rows * lax.axis_size("lat") - RIM
    ids = first + jnp.arange(rows, dtype=jnp.int32)
    keys = labels * 2 + (ids >= last).astype(jnp.int32)[:, None]
    keys = keys.reshape(rows // WIN, WIN, cols // WIN, WIN).transpose(0, 2, 1, 3).reshape(-1, TOK)
    return (
        jnp.broadcast_to(keys.reshape(-1, 1), (keys.size, 128)),
        jnp.concatenate([keys] * 4, 1),
    )


def per_device(
    tokens, region1, region2, bias_index, ln1_gain, qkv_weight1, out_weight1, bias_table1,
    merge_gain, merge_weight, ln2_gain, qkv_weight2, out_weight2, bias_table2, cot_fine, cot_coarse,
):
    rc, cc, feat = tokens.shape
    r2, c2, feat2 = cot_coarse.shape
    heads1, heads2 = bias_table1.shape[1], bias_table2.shape[1]
    entries = bias_table1.shape[0]
    n_tok = rc * cc
    n_win = n_tok // (TOK)
    nr, nc, nk = RIM * cc, rc * RIM, RIM * RIM
    xr, xc, xk = send(
        tokens[:RIM].reshape(nr, feat),
        tokens[:, :RIM].reshape(nc, feat),
        tokens[:RIM, :RIM].reshape(nk, feat),
        -1,
    )
    cr, ccl, ck = send(
        jnp.concatenate([cot_fine[: 2 * RIM].reshape(-1, feat), halves(cot_coarse[:RIM])], 0),
        jnp.concatenate([cot_fine[:, : 2 * RIM].reshape(-1, feat), halves(cot_coarse[:, :RIM])], 0),
        jnp.concatenate(
            [cot_fine[: 2 * RIM, : 2 * RIM].reshape(-1, feat), halves(cot_coarse[:RIM, :RIM])], 0
        ),
        -1,
    )
    key_col1, key_row1 = window_keys(region1)
    key_col2, key_row2 = window_keys(region2)
    tables = jnp.concatenate([bias_table1, bias_table2], 1)
    lookup = (
        bias_index.T.reshape(-1)[:, None] == jnp.arange(entries, dtype=jnp.int32)[None, :]
    ).astype(F32)
    biases = jnp.dot(lookup, tables, precision=lax.Precision.HIGHEST)
    biases = biases.reshape(TOK, TOK, heads1 + heads2).transpose(0, 2, 1)
    bias1 = biases[:, :heads1].reshape(TOK, heads1 * TOK)
    bias2 = biases[:, heads1:].reshape(TOK, heads2 * TOK)
    gain1 = ln1_gain.reshape(1, feat)
    gain2 = ln2_gain.reshape(1, feat2)
    mgain = merge_gain.reshape(1, 4 * feat)

    xw, qkv, mixed, fs, fr, fc, fk = call(
        fine_forward_kernel,
        (
            sds(n_tok, feat), sds(n_tok, 3 * feat), sds(n_tok, feat), sds(rc, cc, feat),
            sds(nr, feat), sds(nc, feat), sds(nk, feat),
        ),
        [(rc + RIM, cc + 2 * RIM, feat), (rc, cc, feat)],
        tokens, xr, xc, xk, key_col1, key_row1, bias1, gain1, qkv_weight1, out_weight1,
    )
    fr, fc, fk = send(fr, fc, fk, -1)
    outs = call(
        coarse_kernel,
        (
            sds(r2, c2, feat2), sds(rc, cc, feat),
            sds(2 * nr, feat), sds(2 * nc, feat), sds(3 * nk, feat),
            sds(1, 4 * feat, dtype=F32), sds(4 * feat, feat2, dtype=F32),
            sds(1, feat2, dtype=F32), sds(feat2, 3 * feat2, dtype=F32),
            sds(feat2, feat2, dtype=F32), sds(TOK, heads2 * TOK, dtype=F32),
        ),
        [
            (rc + RIM, cc + 2 * RIM, feat), (rc + 2 * RIM, cc + 2 * RIM, feat),
            (2, r2 + RIM, c2 + 2 * RIM, feat), (rc, cc, feat), (2, r2, c2, feat),
        ],
        fs, fr, fc, fk,
        cot_fine, cr[: 2 * nr], ccl[: 2 * nc], ck[: 4 * nk],
        cot_coarse, cr[2 * nr :].reshape(2, -1, feat), ccl[2 * nc :].reshape(2, -1, feat),
        ck[4 * nk :].reshape(2, -1, feat),
        key_col2, key_row2, bias2, mgain, merge_weight, gain2, qkv_weight2, out_weight2,
    )
    cs, cfo, er, ec, ek, gmgain, gmerge, ggain2, gqkv2, gout2, gbias2 = outs
    er, ec, ek = send(er, ec, ek, 1)
    back, br, bc, bk, coarse_out, ggain1, gqkv1, gout1, gbias1 = call(
        fine_backward_kernel,
        (
            sds(rc, cc, feat), sds(nr, feat), sds(nc, feat), sds(nk, feat), sds(r2, c2, feat2),
            sds(1, feat, dtype=F32), sds(feat, 3 * feat, dtype=F32), sds(feat, feat, dtype=F32),
            sds(TOK, heads1 * TOK, dtype=F32),
        ),
        [
            (rc + RIM, cc + 2 * RIM, feat), (2, r2 + RIM, c2 + 2 * RIM, feat), (rc, cc, feat), (8, 128),
        ],
        cfo, er[:nr], ec[:nc], ek[:nk],
        cs, er[nr:].reshape(2, -1, feat), ec[nc:].reshape(2, -1, feat), ek[nk:].reshape(2, -1, feat),
        xw, qkv, mixed, key_col1, key_row1, bias1, gain1, qkv_weight1, out_weight1,
    )
    br, bc, bk = send(br, bc, bk, 1)
    grad_tokens = call(
        place_kernel, sds(rc, cc, feat), [(rc + RIM, cc + 2 * RIM, feat)], back, br, bc, bk
    )

    def table_grad(total, heads):
        spread = total.reshape(TOK, heads, TOK).transpose(0, 2, 1).reshape(TOK * TOK, heads)
        return lax.dot_general(
            lookup, spread, (((0,), (0,)), ((), ())), precision=lax.Precision.HIGHEST
        )

    gtable1 = table_grad(gbias1, heads1)
    gtable2 = table_grad(gbias2, heads2)
    summed = lax.psum(
        (ggain1, gqkv1, gout1, gtable1, gmgain, gmerge, ggain2, gqkv2, gout2, gtable2),
        ("lon", "lat"),
    )
    scale = 4.0 / math.sqrt(n_tok * lax.axis_size("lat") * lax.axis_size("lon"))
    s = [v * scale for v in summed]
    return (
        coarse_out, grad_tokens, s[0].reshape(-1), s[1], s[2], s[3], s[4].reshape(-1), s[5],
        s[6].reshape(-1), s[7], s[8], s[9],
    )


def solution(mesh):
    grid = P("lat", "lon", None)
    flat = P("lat", "lon")
    return jax.shard_map(
        per_device,
        mesh=mesh,
        in_specs=(grid, flat, flat) + (P(),) * 11 + (grid, grid),
        out_specs=(grid, grid) + (P(),) * 10,
        check_vma=False,
    )
```

```python
from functools import partial
import math

import jax
import jax.numpy as jnp
from jax import lax
from jax.experimental import pallas as pl
from jax.experimental.pallas import tpu as pltpu
from jax.sharding import PartitionSpec as P

WIN = 8
RIM = 4
TOK = WIN * WIN
EPSILON = 1e-05
MASKED = -1000000000.0
F32 = jnp.float32
BF16 = jnp.bfloat16
VMEM_LIMIT = 24 * 1024 * 1024


def nt_dot(a, b):
    return lax.dot_general(a, b, (((1,), (1,)), ((), ())), preferred_element_type=F32)


def tn_dot(a, b):
    return lax.dot_general(a, b, (((0,), (0,)), ((), ())), preferred_element_type=F32)


def nn_dot(a, b):
    return jnp.dot(a, b, preferred_element_type=F32)


def head_masks():
    rows = lax.broadcasted_iota(jnp.int32, (4 * TOK, 128), 0) // TOK
    lanes = lax.broadcasted_iota(jnp.int32, (4 * TOK, 128), 1) // 32
    return rows == lanes


def spread_heads(part, hm):
    return jnp.where(hm, jnp.concatenate([part] * 4, 0), jnp.zeros((), part.dtype))


def fold_heads(wide, hm):
    kept = jnp.where(hm, wide, 0.0)
    return (kept[:TOK] + kept[TOK : 2 * TOK]) + (kept[2 * TOK : 3 * TOK] + kept[3 * TOK :])


def probs(q4, k, bias, same):
    scores = nt_dot(k, q4) * (32 ** (-0.5)) + bias
    scores = jnp.where(same > 0.5, scores, MASKED)
    top = jnp.max(scores, axis=0, keepdims=True)
    grown = jnp.exp(scores - top)
    return grown * (1.0 / jnp.sum(grown, axis=0, keepdims=True))


def unit_forward(q, k, v, bias, same, hm):
    weights = probs(spread_heads(q, hm), k, bias, same).astype(BF16)
    return fold_heads(tn_dot(weights, v), hm).astype(BF16)


def unit_backward(q, k, v, g, bias, same, hm):
    q4 = spread_heads(q, hm)
    g4 = spread_heads(g, hm)
    p = probs(q4, k, bias, same)
    dp = nt_dot(v, g4).astype(BF16).astype(F32)
    ds = p * (dp - jnp.sum(p * dp, axis=0, keepdims=True))
    dsb = (ds * (32 ** (-0.5))).astype(BF16)
    dq = fold_heads(tn_dot(dsb, k), hm).astype(BF16)
    dk = nn_dot(dsb, q4).astype(BF16)
    dv = nn_dot(p.astype(BF16), g4).astype(BF16)
    return dq, dk, dv, ds


def same_keys(onehot):
    return nt_dot(onehot, jnp.concatenate([onehot] * 4, 0))


def unit_norm(x):
    centered = x - jnp.mean(x, axis=-1, keepdims=True)
    rstd = lax.rsqrt(jnp.mean(centered * centered, axis=-1, keepdims=True) + EPSILON)
    return centered * rstd, rstd


def norm_back(hat, rstd, cot, gain):
    d = cot * gain
    return rstd * (
        d - jnp.mean(d, axis=-1, keepdims=True) - hat * jnp.mean(d * hat, axis=-1, keepdims=True)
    )


def pulled(field, own, rows, cols, corner, rim, rc, cc):
    feat = field.shape[-1]
    field[0:rc, 0:cc] = own.astype(F32)
    field[rc : rc + rim, 0:cc] = rows.astype(F32).reshape(rim, cc, feat)
    field[0:rc, cc : cc + rim] = cols.astype(F32).reshape(rc, rim, feat)
    field[rc : rc + rim, cc : cc + rim] = corner.astype(F32).reshape(rim, rim, feat)


def pushed(field, own, rows, cols, corner, rim, rc, cc):
    feat = field.shape[-1]
    field[rim : rim + rc, rim : rim + cc] = own.astype(F32)
    field[0:rim, rim : rim + cc] = rows.astype(F32).reshape(rim, cc, feat)
    field[rim : rim + rc, 0:rim] = cols.astype(F32).reshape(rc, rim, feat)
    field[0:rim, 0:rim] = corner.astype(F32).reshape(rim, rim, feat)


MISC = 256


def place():
    lat, lon = lax.axis_index("lat"), lax.axis_index("lon")
    return lax.rem(lat, 2), lax.rem(lat // 2, 4), lat // 8 * 2 + lax.rem(lon, 2), lon // 2


def put_rows(packed, half, start, rows):
    count, each = rows.shape[0], packed.shape[2]
    done = 0
    while done < count:
        quarter, offset = divmod(start + done, each)
        take = min(count - done, each - offset)
        packed[half, quarter, offset : offset + take, :] = rows[done : done + take]
        done += take


def table_sums(totals, index, spread):
    lane = lax.broadcasted_iota(jnp.int32, (TOK // 2, 128), 1)
    spread[...] = jnp.zeros(spread.shape, F32)
    head = 0
    for total in totals:
        for p in range(2):
            block = total[:, p * 128 : (p + 1) * 128]
            upper, lower = block[: TOK // 2], block[TOK // 2 :]
            spread[:, head, :] = jnp.where(lane < 64, upper, pltpu.roll(lower, 64, 1))
            spread[:, head + 1, :] = jnp.where(lane < 64, pltpu.roll(upper, 64, 1), lower)
            head += 2
    entry = lax.broadcasted_iota(jnp.int32, (256, 256), 0)
    sums = jnp.zeros((32, 256), F32)
    for q in range(TOK // 4):
        part = jnp.concatenate([spread[2 * q], spread[2 * q + 1]], 1)
        high = part.astype(BF16)
        low = (part - high.astype(F32)).astype(BF16)
        at = jnp.concatenate([index[2 * q : 2 * q + 1, :], index[2 * q + 1 : 2 * q + 2, :]], 1)
        chosen = jnp.where(entry == at, 1.0, 0.0).astype(BF16)
        sums = sums + nt_dot(jnp.concatenate([high, low], 0), chosen)
    return sums[:16] + sums[16:]


def strips_kernel(x, row_out, col_out, corner_out):
    rc, cc, feat = x.shape
    row_out[...] = x[0:RIM].reshape(RIM * cc, feat)
    cols = x[:, 0:16, :].astype(F32)[:, :RIM]
    col_out[...] = cols.reshape(rc * RIM, feat).astype(BF16)
    corner_out[...] = cols[:RIM].reshape(RIM * RIM, feat).astype(BF16)


def prepare_kernel(
    cf, cc2, region1, region2, index, table1, table2,
    row_out, col_out, corner_out, keys1, keys2, bias1, bias2, pairs_out,
    tables,
):
    rc, cc, feat = cf.shape
    r2, c2, _ = cc2.shape
    nr, nc, nk = RIM * cc, rc * RIM, RIM * RIM
    row_out[0 : 2 * nr] = cf[0 : 2 * RIM].reshape(2 * nr, feat)
    cols = cf[:, 0:16, :].astype(F32)[:, : 2 * RIM]
    col_out[0 : 2 * nc] = cols.reshape(2 * nc, feat).astype(BF16)
    corner_out[0 : 4 * nk] = cols[: 2 * RIM].reshape(4 * nk, feat).astype(BF16)
    cols = cc2[:, 0:16, :].astype(F32)[:, :RIM]
    for half in range(2):
        lanes = slice(half * feat, (half + 1) * feat)
        row_out[2 * nr + half * nr // 2 : 2 * nr + (half + 1) * nr // 2] = cc2[
            0:RIM, :, lanes
        ].reshape(nr // 2, feat)
        part = cols[:, :, lanes]
        col_out[2 * nc + half * nc // 2 : 2 * nc + (half + 1) * nc // 2] = part.reshape(
            nc // 2, feat
        ).astype(BF16)
        corner_out[4 * nk + half * nk : 4 * nk + (half + 1) * nk] = (
            part[:RIM].reshape(nk, feat).astype(BF16)
        )
    last = lax.axis_index("lat") == lax.axis_size("lat") - 1
    token = lax.broadcasted_iota(jnp.int32, (TOK, 128), 0)
    lane = lax.broadcasted_iota(jnp.int32, (TOK, 128), 1)
    for region, out in ((region1, keys1), (region2, keys2)):
        rows, columns = region.shape
        labels = jnp.broadcast_to(region[...][:, :, None], (rows, columns, 128))
        w = 0
        for a in range(rows // WIN):
            for b in range(columns // WIN):
                key = 2 * labels[WIN * a : WIN * (a + 1), WIN * b : WIN * (b + 1)].reshape(TOK, 128)
                if a == rows // WIN - 1:
                    key = key + jnp.where(
                        jnp.logical_and(last, token >= RIM * WIN), 1, 0
                    )
                out[w * TOK : (w + 1) * TOK, :] = jnp.where(key == lane, 1.0, 0.0).astype(BF16)
                w += 1
    tables[...] = jnp.zeros(tables.shape, F32)
    h1, entries = table1.shape
    h2 = table2.shape[0]
    tables[0:h1, 0:entries] = table1[...]
    tables[8 : 8 + h2, 0:entries] = table2[...]
    turned = index[...].T
    at = jnp.concatenate([turned, turned], 1)
    pairs_out[...] = jnp.concatenate([turned[: TOK // 2], turned[TOK // 2 :]], 1)
    small = jnp.bitwise_and(at, 127)

    def looked_up(h):
        found = [
            jnp.take_along_axis(
                jnp.broadcast_to(tables[h : h + 1, p * 128 : (p + 1) * 128], (TOK, 128)), small, axis=1
            )
            for p in range(2)
        ]
        return jnp.where(at < 128, found[0], found[1])

    for out, base, heads in ((bias1, 0, h1), (bias2, 8, h2)):
        for p in range(heads // 2):
            out[:, p * 128 : (p + 1) * 128] = jnp.where(
                lane < 64, looked_up(base + 2 * p), looked_up(base + 2 * p + 1)
            )


def cores_kernel(keep_c, got_c, keep_f, got_f, keep_out, one, two, three):
    x = place()[1]
    for m, out in enumerate((keep_out, one, two, three)):
        part = jnp.concatenate(
            [keep_c[x ^ m] + got_c[x ^ m], keep_f[x ^ m] + got_f[x ^ m]], 0
        )
        out[...] = part.astype(out.dtype)


def rows_kernel(keep, r1, r2, r3, keep_out, one, two, three, total):
    y = place()[2]
    total[...] = (keep[...] + r1[...].astype(F32)) + (r2[...].astype(F32) + r3[...].astype(F32))
    count = keep_out.shape[0]
    for m, out in enumerate((keep_out, one, two, three)):
        out[...] = total[pl.ds(pl.multiple_of((y ^ m) * count, 8), count), :]


def sum_kernel(keep, r1, r2, r3, out):
    out[...] = (keep[...] + r1[...]) + (r2[...] + r3[...])


def finish_kernel(scale, keep, r1, r2, r3, r4, r5, r6, r7, out):
    total = ((keep[...] + r1[...]) + (r2[...] + r3[...])) + (
        (r4[...] + r5[...]) + (r6[...] + r7[...])
    )
    out[...] = (total * scale).astype(BF16)


def gather_kernel(axis, own, r1, r2, r3, out, field):
    at = place()[axis]
    count = own.shape[0]
    for m, part in enumerate((own, r1, r2, r3)):
        field[pl.ds(pl.multiple_of((at ^ m) * count, 8), count), :] = part[...].astype(F32)
    out[...] = field[...].astype(BF16)


def unpack_kernel(own, got, gain1, qkv1, out1, table1, mgain, merge, gain2, qkv2, out2, table2, field):
    core = place()[0]
    field[core] = own[...].astype(F32)
    field[1 - core] = got[...].astype(F32)
    feat = out1.shape[0]
    feat2 = out2.shape[0]
    coarse = 4 * feat * feat2 * 6 // feat // 16
    fine = (4 * feat + MISC) // 8
    each = coarse + fine

    def take(half, start, count, size, base):
        parts, done = [], 0
        while done < count:
            quarter, offset = divmod(start + done, size)
            n = min(count - done, size - offset)
            r0 = quarter * each + base + offset
            parts.append(field[half, r0 : r0 + n, :])
            done += n
        return parts[0] if len(parts) == 1 else jnp.concatenate(parts, 0)

    for b in range(6):
        qkv2[:, b * feat : (b + 1) * feat] = take(0, b * feat2, feat2, coarse, 0)
    for b in range(2):
        out2[:, b * feat : (b + 1) * feat] = take(1, b * feat2, feat2, coarse, 0)
        merge[:, b * feat : (b + 1) * feat] = take(
            1, 2 * feat2 + b * 4 * feat, 4 * feat, coarse, 0
        )
    for b in range(3):
        qkv1[:, b * feat : (b + 1) * feat] = take(0, b * feat, feat, fine, coarse)
    out1[...] = take(1, 0, feat, fine, coarse)
    tables = jnp.concatenate([take(1, feat + 16 * p, 16, fine, coarse) for p in range(2)], 1)
    h1, entries = table1.shape
    h2 = table2.shape[0]
    table1[...] = tables[0:h1, 0:entries]
    table2[...] = tables[h1 : h1 + h2, 0:entries]
    gains = take(1, feat + 32, 8, fine, coarse)
    gain1[...] = gains[0:1]
    for q in range(4):
        mgain[:, q * feat : (q + 1) * feat] = gains[1 + q : 2 + q]
    for q in range(2):
        gain2[:, q * feat : (q + 1) * feat] = gains[5 + q : 6 + q]


def fine_forward_kernel(
    x, xr, xc, xk, keys, bias, gain, wqkv, wout,
    xw_out, qkv_out, mixed_out, own_out, row_out, col_out, corner_out,
    field, grid,
):
    rc, cc, feat = x.shape
    pulled(field, x[...], xr[...], xc[...], xk[...], RIM, rc, cc)
    hm = head_masks()
    wide = cc // WIN
    group = 4
    for a in range(rc // WIN):
        for b0 in range(0, wide, group):
            r0 = RIM + WIN * a
            parts = [
                field[r0 : r0 + WIN, RIM + WIN * b : RIM + WIN * (b + 1), :].reshape(TOK, feat)
                for b in range(b0, b0 + group)
            ]
            tokens = jnp.concatenate(parts, 0)
            t0 = (a * wide + b0) * TOK
            span = pl.ds(t0, group * TOK)
            xw_out[span, :] = tokens.astype(BF16)
            hat, _ = unit_norm(tokens)
            normed = (hat * gain[...]).astype(BF16)
            qkv = nn_dot(normed, wqkv[...]).astype(BF16)
            qkv_out[span, :] = qkv
            mixed = []
            for n in range(group):
                w = a * wide + b0 + n
                rows = slice(n * TOK, (n + 1) * TOK)
                mixed.append(
                    unit_forward(
                        qkv[rows, :feat],
                        qkv[rows, feat : 2 * feat],
                        qkv[rows, 2 * feat :],
                        bias[...],
                        same_keys(keys[w * TOK : (w + 1) * TOK, :]),
                        hm,
                    )
                )
            mixed = jnp.concatenate(mixed, 0)
            mixed_out[span, :] = mixed
            result = tokens + nn_dot(mixed, wout[...])
            for n in range(group):
                b = b0 + n
                grid[WIN * a : WIN * (a + 1), WIN * b : WIN * (b + 1), :] = result[
                    n * TOK : (n + 1) * TOK
                ].reshape(WIN, WIN, feat)
    own_out[...] = grid[...].astype(BF16)
    row_out[...] = grid[0:RIM].reshape(RIM * cc, feat).astype(BF16)
    col_out[...] = grid[:, 0:RIM].reshape(rc * RIM, feat).astype(BF16)
    corner_out[...] = grid[0:RIM, 0:RIM].reshape(RIM * RIM, feat).astype(BF16)


def coarse_kernel(
    f, fr, fc, fk, cf, cc2, cr, ccl, ck,
    keys, bias, mgain, wmerge, gain, wqkv, wout,
    own_out, fine_out, row_out, col_out, corner_out,
    send_out, keep_out, gmgain, ggain, gbias,
    field, cfield, coarse_field, fgrid, cgrid, packed,
):
    rc, cc, feat = f.shape
    r2, c2 = rc // 2, cc // 2
    feat2 = 2 * feat
    wide = c2 // WIN
    windows = [(a, b) for a in range(r2 // WIN) for b in range(wide)]
    count = len(windows) * TOK
    hm = head_masks()
    pulled(field, f[...], fr[...], fc[...], fk[...], RIM, rc, cc)
    nr, nc, nk = RIM * cc, rc * RIM, RIM * RIM
    pulled(cfield, cf[...], cr[: 2 * nr], ccl[: 2 * nc], ck[: 4 * nk], 2 * RIM, rc, cc)
    for half in range(2):
        lanes = slice(half * feat, (half + 1) * feat)
        pulled(
            coarse_field.at[half],
            cc2[:, :, lanes],
            cr[pl.ds(2 * nr + half * nr // 2, nr // 2)],
            ccl[pl.ds(2 * nc + half * nc // 2, nc // 2)],
            ck[pl.ds(4 * nk + half * nk, nk)],
            RIM,
            r2,
            c2,
        )

    def in_windows(load):
        return jnp.concatenate([load(a, b).reshape(TOK, feat) for a, b in windows], 0)

    def joined_part(ref, rim, quad):
        dc, dr = quad // 2, quad % 2

        def load(a, b):
            return jnp.stack(
                [
                    ref[
                        rim + 2 * (WIN * a + r) + dr,
                        pl.ds(rim + 2 * WIN * b + dc, WIN, stride=2),
                        :,
                    ]
                    for r in range(WIN)
                ],
                0,
            )

        return in_windows(load)

    parts = [joined_part(field, RIM, quad) for quad in range(4)]
    mean = sum(jnp.sum(p, axis=-1, keepdims=True) for p in parts) * (1.0 / (4 * feat))
    centered = [p - mean for p in parts]
    spread = sum(jnp.sum(p * p, axis=-1, keepdims=True) for p in centered) * (1.0 / (4 * feat))
    mrstd = lax.rsqrt(spread + EPSILON)
    mhat = [p * mrstd for p in centered]
    mgains = [mgain[:, q * feat : (q + 1) * feat] for q in range(4)]
    mnormed = jnp.concatenate([(h * g).astype(BF16) for h, g in zip(mhat, mgains)], 1)
    coarse_in = nn_dot(mnormed, wmerge[...]).astype(BF16).astype(F32)
    hat, rstd = unit_norm(coarse_in)
    normed = (hat * gain[...]).astype(BF16)
    qkv = nn_dot(normed, wqkv[...]).astype(BF16)
    mixed = []
    for w in range(len(windows)):
        rows = slice(w * TOK, (w + 1) * TOK)
        units = []
        same = same_keys(keys[rows, :])
        for g in range(2):
            lo = g * feat
            units.append(
                unit_forward(
                    qkv[rows, lo : lo + feat],
                    qkv[rows, feat2 + lo : feat2 + lo + feat],
                    qkv[rows, 2 * feat2 + lo : 2 * feat2 + lo + feat],
                    bias[:, g * 4 * TOK : (g + 1) * 4 * TOK],
                    same,
                    hm,
                )
            )
        mixed.append(jnp.concatenate(units, 1))
    mixed = jnp.concatenate(mixed, 0)
    result = coarse_in + nn_dot(mixed, wout[...])
    for w, (a, b) in enumerate(windows):
        for half in range(2):
            cgrid[half, WIN * a : WIN * (a + 1), WIN * b : WIN * (b + 1), :] = result[
                w * TOK : (w + 1) * TOK, half * feat : (half + 1) * feat
            ].reshape(WIN, WIN, feat)
    cot = jnp.concatenate(
        [
            in_windows(
                lambda a, b: coarse_field[
                    half,
                    RIM + WIN * a : RIM + WIN * (a + 1),
                    RIM + WIN * b : RIM + WIN * (b + 1),
                    :,
                ]
            )
            for half in range(2)
        ],
        1,
    )
    cotb = cot.astype(BF16)
    grad = tn_dot(mixed, cotb)
    for b in range(2):
        put_rows(packed, 1, b * feat2, grad[:, b * feat : (b + 1) * feat])
    cot_mixed = nt_dot(cotb, wout[...]).astype(BF16)
    cot_rows = []
    total = [jnp.zeros((TOK, 4 * TOK), F32) for _ in range(2)]
    for w in range(len(windows)):
        rows = slice(w * TOK, (w + 1) * TOK)
        dqs, dks, dvs = [], [], []
        same = same_keys(keys[rows, :])
        for g in range(2):
            lo = g * feat
            dq, dk, dv, ds = unit_backward(
                qkv[rows, lo : lo + feat],
                qkv[rows, feat2 + lo : feat2 + lo + feat],
                qkv[rows, 2 * feat2 + lo : 2 * feat2 + lo + feat],
                cot_mixed[rows, lo : lo + feat],
                bias[:, g * 4 * TOK : (g + 1) * 4 * TOK],
                same,
                hm,
            )
            dqs.append(dq)
            dks.append(dk)
            dvs.append(dv)
            total[g] = total[g] + ds
        cot_rows.append(jnp.concatenate(dqs + dks + dvs, 1))
    gbias[...] = jnp.concatenate(total, 1)
    cot_qkv = jnp.concatenate(cot_rows, 0)
    grad = tn_dot(normed, cot_qkv)
    for b in range(6):
        put_rows(packed, 0, b * feat2, grad[:, b * feat : (b + 1) * feat])
    cot_unit = nt_dot(cot_qkv, wqkv[...]).astype(BF16).astype(F32)
    ggain[...] = jnp.sum(cot_unit * hat, axis=0, keepdims=True)
    cot_in = (cot + norm_back(hat, rstd, cot_unit, gain[...])).astype(BF16)
    grad = tn_dot(mnormed, cot_in)
    for b in range(2):
        put_rows(packed, 1, 2 * feat2 + b * 4 * feat, grad[:, b * feat : (b + 1) * feat])
    core = place()[0]
    send_out[...] = packed[1 - core]
    keep_out[...] = packed[core]
    cot_norm = nt_dot(cot_in, wmerge[...]).astype(BF16).astype(F32)
    cot_parts = [cot_norm[:, q * feat : (q + 1) * feat] for q in range(4)]
    gmgain[...] = jnp.concatenate(
        [jnp.sum(c * h, axis=0, keepdims=True) for c, h in zip(cot_parts, mhat)], 1
    )
    ds = [c * g for c, g in zip(cot_parts, mgains)]
    mean_d = sum(jnp.sum(d, axis=-1, keepdims=True) for d in ds) * (1.0 / (4 * feat))
    mean_dh = sum(jnp.sum(d * h, axis=-1, keepdims=True) for d, h in zip(ds, mhat)) * (
        1.0 / (4 * feat)
    )
    for quad in range(4):
        dc, dr = quad // 2, quad % 2
        back = mrstd * (ds[quad] - mean_d - mhat[quad] * mean_dh)
        back = back + joined_part(cfield, 2 * RIM, quad)
        for w, (a, b) in enumerate(windows):
            for r in range(WIN):
                t0 = w * TOK + r * WIN
                fgrid[
                    2 * (WIN * a + r) + dr, pl.ds(2 * WIN * b + dc, WIN, stride=2), :
                ] = back[t0 : t0 + WIN]
    own_out[...] = jnp.concatenate([cgrid[0], cgrid[1]], -1).astype(BF16)
    fine_out[...] = fgrid[...].astype(BF16)
    row_out[0:nr] = fgrid[rc - RIM :].reshape(nr, feat).astype(BF16)
    col_out[0:nc] = fgrid[:, cc - RIM :].reshape(nc, feat).astype(BF16)
    corner_out[0:nk] = fgrid[rc - RIM :, cc - RIM :].reshape(nk, feat).astype(BF16)
    for half in range(2):
        row_out[nr + half * nr // 2 : nr + (half + 1) * nr // 2] = (
            cgrid[half, r2 - RIM :].reshape(nr // 2, feat).astype(BF16)
        )
        col_out[nc + half * nc // 2 : nc + (half + 1) * nc // 2] = (
            cgrid[half, :, c2 - RIM :].reshape(nc // 2, feat).astype(BF16)
        )
        corner_out[nk + half * nk : nk + (half + 1) * nk] = (
            cgrid[half, r2 - RIM :, c2 - RIM :].reshape(nk, feat).astype(BF16)
        )


def fine_backward_kernel(
    c, d, er, ec, ek, xw, qkv_in, mixed_in, keys, bias, gain, wqkv, wout,
    gmgain, ggain2, gbias2, index,
    own_out, row_out, col_out, corner_out, coarse_out, send_out, keep_out,
    field, dfield, grid, packed, spread,
):
    rc, cc, feat = c.shape
    r2, c2 = rc // 2, cc // 2
    nr, nc, nk = RIM * cc, rc * RIM, RIM * RIM
    pushed(field, c[...], er[:nr], ec[:nc], ek[:nk], RIM, rc, cc)
    for half in range(2):
        lanes = slice(half * feat, (half + 1) * feat)
        pushed(
            dfield.at[half],
            d[:, :, lanes],
            er[pl.ds(nr + half * nr // 2, nr // 2)],
            ec[pl.ds(nc + half * nc // 2, nc // 2)],
            ek[pl.ds(nk + half * nk, nk)],
            RIM,
            r2,
            c2,
        )
        coarse_out[:, :, lanes] = dfield[half, 0:r2, 0:c2].astype(BF16)
    hm = head_masks()
    wide = cc // WIN
    group = 4
    total = jnp.zeros((TOK, 4 * TOK), F32)
    total_gain = jnp.zeros((1, feat), F32)
    total_out = jnp.zeros((feat, feat), F32)
    total_qkv = jnp.zeros((feat, 3 * feat), F32)
    for a in range(rc // WIN):
        for b0 in range(0, wide, group):
            cot = jnp.concatenate(
                [
                    field[
                        WIN * a : WIN * (a + 1), WIN * b : WIN * (b + 1), :
                    ].reshape(TOK, feat)
                    for b in range(b0, b0 + group)
                ],
                0,
            )
            t0 = (a * wide + b0) * TOK
            span = pl.ds(t0, group * TOK)
            cotb = cot.astype(BF16)
            total_out = total_out + tn_dot(mixed_in[span, :], cotb)
            cot_mixed = nt_dot(cotb, wout[...]).astype(BF16)
            qkv = qkv_in[span, :]
            cot_rows = []
            for n in range(group):
                w = a * wide + b0 + n
                rows = slice(n * TOK, (n + 1) * TOK)
                dq, dk, dv, ds = unit_backward(
                    qkv[rows, :feat],
                    qkv[rows, feat : 2 * feat],
                    qkv[rows, 2 * feat :],
                    cot_mixed[rows],
                    bias[...],
                    same_keys(keys[w * TOK : (w + 1) * TOK, :]),
                    hm,
                )
                total = total + ds
                cot_rows.append(jnp.concatenate([dq, dk, dv], 1))
            cot_qkv = jnp.concatenate(cot_rows, 0)
            hat, rstd = unit_norm(xw[span, :].astype(F32))
            normed = (hat * gain[...]).astype(BF16)
            total_qkv = total_qkv + tn_dot(normed, cot_qkv)
            cot_unit = nt_dot(cot_qkv, wqkv[...]).astype(BF16).astype(F32)
            total_gain = total_gain + jnp.sum(cot_unit * hat, axis=0, keepdims=True)
            result = cot + norm_back(hat, rstd, cot_unit, gain[...])
            for n in range(group):
                b = b0 + n
                grid[WIN * a : WIN * (a + 1), WIN * b : WIN * (b + 1), :] = result[
                    n * TOK : (n + 1) * TOK
                ].reshape(WIN, WIN, feat)
    for b in range(3):
        put_rows(packed, 0, b * feat, total_qkv[:, b * feat : (b + 1) * feat])
    put_rows(packed, 1, 0, total_out)
    tables = table_sums([total, gbias2[:, : 4 * TOK], gbias2[:, 4 * TOK :]], index, spread)
    gains = jnp.concatenate(
        [total_gain]
        + [gmgain[:, q * feat : (q + 1) * feat] for q in range(4)]
        + [ggain2[:, q * feat : (q + 1) * feat] for q in range(2)]
        + [jnp.zeros((1, feat), F32)],
        0,
    )
    rest = jnp.zeros((MISC - 40, feat), F32)
    put_rows(
        packed, 1, feat, jnp.concatenate([tables[:, :feat], tables[:, feat:], gains, rest], 0)
    )
    core = place()[0]
    send_out[...] = packed[1 - core]
    keep_out[...] = packed[core]
    own_out[...] = grid[...].astype(BF16)
    row_out[...] = grid[rc - RIM :].reshape(nr, feat).astype(BF16)
    col_out[...] = grid[:, cc - RIM :].reshape(nc, feat).astype(BF16)
    corner_out[...] = grid[rc - RIM :, cc - RIM :].reshape(nk, feat).astype(BF16)


def place_kernel(c, cr, cc_, ck, out, field):
    rc, cc, _ = c.shape
    pushed(field, c[...], cr[...], cc_[...], ck[...], RIM, rc, cc)
    out[...] = field[0:rc, 0:cc].astype(BF16)


def call(kernel, outs, scratch, *args):
    return pl.pallas_call(
        kernel,
        out_shape=outs,
        scratch_shapes=[pltpu.VMEM(s, F32) for s in scratch],
        compiler_params=pltpu.CompilerParams(vmem_limit_bytes=VMEM_LIMIT),
    )(*args)


def sds(*shape, dtype=BF16):
    return jax.ShapeDtypeStruct(shape, dtype)


def send(rows, cols, corner, sense):
    nlat, nlon = lax.axis_size("lat"), lax.axis_size("lon")
    lat = [(i, (i + sense) % nlat) for i in range(nlat)]
    lon = [(i, (i + sense) % nlon) for i in range(nlon)]
    both = [
        (j * nlat + i, (j + sense) % nlon * nlat + (i + sense) % nlat)
        for i in range(nlat)
        for j in range(nlon)
    ]
    return (
        lax.ppermute(rows, "lat", lat),
        lax.ppermute(cols, "lon", lon),
        lax.ppermute(corner, ("lon", "lat"), both),
    )


def flipped(value, lat_bits, lon_bits):
    nlat, nlon = lax.axis_size("lat"), lax.axis_size("lon")
    if not lon_bits:
        return lax.ppermute(value, "lat", [(i, i ^ lat_bits) for i in range(nlat)])
    if not lat_bits:
        return lax.ppermute(value, "lon", [(j, j ^ lon_bits) for j in range(nlon)])
    pairs = [
        (j * nlat + i, (j ^ lon_bits) * nlat + (i ^ lat_bits))
        for j in range(nlon)
        for i in range(nlat)
    ]
    return lax.ppermute(value, ("lon", "lat"), pairs)


def along_x(values):
    return [flipped(v, 2 * m, 0) for m, v in zip((1, 2, 3), values)]


def along_y(values):
    return [flipped(v, 8 * (m // 2), m % 2) for m, v in zip((1, 2, 3), values)]


def per_device(
    tokens, region1, region2, bias_index, ln1_gain, qkv_weight1, out_weight1, bias_table1,
    merge_gain, merge_weight, ln2_gain, qkv_weight2, out_weight2, bias_table2, cot_fine, cot_coarse,
):
    rc, cc, feat = tokens.shape
    r2, c2, feat2 = cot_coarse.shape
    heads1, heads2 = bias_table1.shape[1], bias_table2.shape[1]
    entries = bias_table1.shape[0]
    n_tok = rc * cc
    nr, nc, nk = RIM * cc, rc * RIM, RIM * RIM
    coarse_rows = 4 * feat * feat2 * 6 // feat // 16
    fine_rows = (4 * feat + MISC) // 8
    each = coarse_rows + fine_rows
    gain1 = ln1_gain.reshape(1, feat)
    gain2 = ln2_gain.reshape(1, feat2)
    mgain = merge_gain.reshape(1, 4 * feat)
    f32 = partial(sds, dtype=F32)

    strips = call(strips_kernel, (sds(nr, feat), sds(nc, feat), sds(nk, feat)), [], tokens)
    xr, xc, xk = send(*strips, -1)
    cr, ccl, ck, keys1, keys2, bias1, bias2, pairs = call(
        prepare_kernel,
        (
            sds(3 * nr, feat), sds(3 * nc, feat), sds(6 * nk, feat),
            sds(n_tok, 128), sds(n_tok // 4, 128), f32(TOK, heads1 * TOK), f32(TOK, heads2 * TOK),
            sds(TOK // 2, 2 * TOK, dtype=jnp.int32),
        ),
        [(16, 256)],
        cot_fine, cot_coarse, region1, region2, bias_index, bias_table1.T, bias_table2.T,
    )
    cr, ccl, ck = send(cr, ccl, ck, -1)
    xw, qkv, mixed, fs, fr, fc, fk = call(
        fine_forward_kernel,
        (
            sds(n_tok, feat), sds(n_tok, 3 * feat), sds(n_tok, feat), sds(rc, cc, feat),
            sds(nr, feat), sds(nc, feat), sds(nk, feat),
        ),
        [(rc + RIM, cc + 2 * RIM, feat), (rc, cc, feat)],
        tokens, xr, xc, xk, keys1, bias1, gain1, qkv_weight1, out_weight1,
    )
    fr, fc, fk = send(fr, fc, fk, -1)
    cs, cfo, er, ec, ek, send_c, keep_c, gmgain, ggain2, gbias2 = call(
        coarse_kernel,
        (
            sds(r2, c2, feat2), sds(rc, cc, feat),
            sds(2 * nr, feat), sds(2 * nc, feat), sds(3 * nk, feat),
            f32(4, coarse_rows, feat), f32(4, coarse_rows, feat),
            f32(1, 4 * feat), f32(1, feat2), f32(TOK, heads2 * TOK),
        ),
        [
            (rc + RIM, cc + 2 * RIM, feat), (rc + 2 * RIM, cc + 2 * RIM, feat),
            (2, r2 + RIM, c2 + 2 * RIM, feat), (rc, cc, feat), (2, r2, c2, feat),
            (2, 4, coarse_rows, feat),
        ],
        fs, fr, fc, fk, cot_fine, cot_coarse, cr, ccl, ck,
        keys2, bias2, mgain, merge_weight, gain2, qkv_weight2, out_weight2,
    )
    er, ec, ek = send(er, ec, ek, 1)
    got_c = flipped(send_c, 1, 0)
    back, br, bc, bk, coarse_out, send_f, keep_f = call(
        fine_backward_kernel,
        (
            sds(rc, cc, feat), sds(nr, feat), sds(nc, feat), sds(nk, feat), sds(r2, c2, feat2),
            f32(4, fine_rows, feat), f32(4, fine_rows, feat),
        ),
        [
            (rc + RIM, cc + 2 * RIM, feat), (2, r2 + RIM, c2 + 2 * RIM, feat), (rc, cc, feat),
            (2, 4, fine_rows, feat), (TOK // 2, 16, 128),
        ],
        cfo, cs, er, ec, ek, xw, qkv, mixed, keys1, bias1, gain1, qkv_weight1, out_weight1,
        gmgain, ggain2, gbias2, pairs,
    )
    got_f = flipped(send_f, 1, 0)
    br, bc, bk = send(br, bc, bk, 1)
    keep, *out = call(
        cores_kernel, (f32(each, feat),) + (sds(each, feat),) * 3, [], keep_c, got_c, keep_f, got_f
    )
    keep, *out = call(
        rows_kernel, (f32(each // 4, feat),) * 4, [(each, feat)], keep, *along_x(out)
    )
    part = call(sum_kernel, f32(each // 4, feat), [], keep, *along_y(out))
    grad_tokens = call(
        place_kernel, sds(rc, cc, feat), [(rc + RIM, cc + 2 * RIM, feat)], back, br, bc, bk
    )
    scale = 4.0 / math.sqrt(n_tok * lax.axis_size("lat") * lax.axis_size("lon"))
    part = call(
        partial(finish_kernel, scale), sds(each // 4, feat), [],
        part, *[flipped(part, 0, 2 * m) for m in range(1, 8)],
    )
    part = call(
        partial(gather_kernel, 2), sds(each, feat), [(each, feat)], part, *along_y([part] * 3)
    )
    part = call(
        partial(gather_kernel, 1), sds(4 * each, feat), [(4 * each, feat)], part, *along_x([part] * 3)
    )
    g = call(
        unpack_kernel,
        (
            f32(1, feat), f32(feat, 3 * feat), f32(feat, feat), f32(heads1, entries),
            f32(1, 4 * feat), f32(4 * feat, feat2), f32(1, feat2), f32(feat2, 3 * feat2),
            f32(feat2, feat2), f32(heads2, entries),
        ),
        [(2, 4 * each, feat)],
        part, flipped(part, 1, 0),
    )
    return (
        coarse_out, grad_tokens, g[0].reshape(-1), g[1], g[2], g[3].T, g[4].reshape(-1), g[5],
        g[6].reshape(-1), g[7], g[8], g[9].T,
    )


def solution(mesh):
    grid = P("lat", "lon", None)
    flat = P("lat", "lon")
    return jax.shard_map(
        per_device,
        mesh=mesh,
        in_specs=(grid, flat, flat) + (P(),) * 11 + (grid, grid),
        out_specs=(grid, grid) + (P(),) * 10,
        check_vma=False,
    )
```

```python
from functools import partial
import math

import jax
import jax.numpy as jnp
from jax import lax
from jax.experimental import pallas as pl
from jax.experimental.pallas import tpu as pltpu
from jax.sharding import PartitionSpec as P

WIN = 8
RIM = 4
TOK = WIN * WIN
EPSILON = 1e-05
MASKED = -1000000000.0
F32 = jnp.float32
BF16 = jnp.bfloat16
LON = ("z", "yl")
LAT = ("yh", "x", "c")
CHIPS = ("z", "yl", "yh", "x")
VMEM_LIMIT = 24 * 1024 * 1024


def nt_dot(a, b):
    return lax.dot_general(a, b, (((1,), (1,)), ((), ())), preferred_element_type=F32)


def tn_dot(a, b):
    return lax.dot_general(a, b, (((0,), (0,)), ((), ())), preferred_element_type=F32)


def nn_dot(a, b):
    return jnp.dot(a, b, preferred_element_type=F32)


def head_masks():
    rows = lax.broadcasted_iota(jnp.int32, (4 * TOK, 128), 0) // TOK
    lanes = lax.broadcasted_iota(jnp.int32, (4 * TOK, 128), 1) // 32
    return rows == lanes


def spread_heads(part, hm):
    return jnp.where(hm, jnp.concatenate([part] * 4, 0), jnp.zeros((), part.dtype))


def fold_heads(wide, hm):
    kept = jnp.where(hm, wide, 0.0)
    return (kept[:TOK] + kept[TOK : 2 * TOK]) + (kept[2 * TOK : 3 * TOK] + kept[3 * TOK :])


def probs(q4, k, bias, same):
    scores = nt_dot(k, q4) * (32 ** (-0.5)) + bias
    scores = jnp.where(jnp.concatenate([same, same], 1) > 0.5, scores, MASKED)
    top = jnp.max(scores, axis=0, keepdims=True)
    grown = jnp.exp(scores - top)
    return grown * (1.0 / jnp.sum(grown, axis=0, keepdims=True))


def unit_forward(q, k, v, bias, same, hm):
    weights = probs(spread_heads(q, hm), k, bias, same).astype(BF16)
    return fold_heads(tn_dot(weights, v), hm).astype(BF16)


def unit_backward(q, k, v, g, bias, same, hm):
    q4 = spread_heads(q, hm)
    g4 = spread_heads(g, hm)
    p = probs(q4, k, bias, same)
    dp = nt_dot(v, g4).astype(BF16).astype(F32)
    ds = p * (dp - jnp.sum(p * dp, axis=0, keepdims=True))
    dsb = (ds * (32 ** (-0.5))).astype(BF16)
    dq = fold_heads(tn_dot(dsb, k), hm).astype(BF16)
    dk = nn_dot(dsb, q4).astype(BF16)
    dv = nn_dot(p.astype(BF16), g4).astype(BF16)
    return dq, dk, dv, ds


def same_keys(onehot):
    return nt_dot(onehot, jnp.concatenate([onehot] * 2, 0))


def unit_norm(x):
    centered = x - jnp.mean(x, axis=-1, keepdims=True)
    rstd = lax.rsqrt(jnp.mean(centered * centered, axis=-1, keepdims=True) + EPSILON)
    return centered * rstd, rstd


def norm_back(hat, rstd, cot, gain):
    d = cot * gain
    return rstd * (
        d - jnp.mean(d, axis=-1, keepdims=True) - hat * jnp.mean(d * hat, axis=-1, keepdims=True)
    )


def pulled(field, own, rows, cols, corner, rim, rc, cc):
    feat = field.shape[-1]
    field[0:rc, 0:cc] = own.astype(F32)
    field[rc : rc + rim, 0:cc] = rows.astype(F32).reshape(rim, cc, feat)
    field[0:rc, cc : cc + rim] = cols.astype(F32).reshape(rc, rim, feat)
    field[rc : rc + rim, cc : cc + rim] = corner.astype(F32).reshape(rim, rim, feat)


def pushed(field, own, rows, cols, corner, rim, rc, cc):
    feat = field.shape[-1]
    field[rim : rim + rc, rim : rim + cc] = own.astype(F32)
    field[0:rim, rim : rim + cc] = rows.astype(F32).reshape(rim, cc, feat)
    field[rim : rim + rc, 0:rim] = cols.astype(F32).reshape(rc, rim, feat)
    field[0:rim, 0:rim] = corner.astype(F32).reshape(rim, rim, feat)


HALF = 2048
COARSE = 1536


def other_core():
    return 1 - lax.axis_index("c")


def table_sums(totals, index, spread):
    lane = lax.broadcasted_iota(jnp.int32, (TOK // 2, 128), 1)
    spread[...] = jnp.zeros(spread.shape, F32)
    head = 0
    for total in totals:
        for p in range(2):
            block = total[:, p * 128 : (p + 1) * 128]
            upper, lower = block[: TOK // 2], block[TOK // 2 :]
            spread[:, head, :] = jnp.where(lane < 64, upper, pltpu.roll(lower, 64, 1))
            spread[:, head + 1, :] = jnp.where(lane < 64, pltpu.roll(upper, 64, 1), lower)
            head += 2
    entry = lax.broadcasted_iota(jnp.int32, (256, 256), 0)
    sums = jnp.zeros((32, 256), F32)
    for q in range(TOK // 4):
        part = jnp.concatenate([spread[2 * q], spread[2 * q + 1]], 1)
        high = part.astype(BF16)
        low = (part - high.astype(F32)).astype(BF16)
        at = jnp.concatenate([index[2 * q : 2 * q + 1, :], index[2 * q + 1 : 2 * q + 2, :]], 1)
        chosen = jnp.where(entry == at, 1.0, 0.0).astype(BF16)
        sums = sums + nt_dot(jnp.concatenate([high, low], 0), chosen)
    return sums[:16] + sums[16:]


def fetch(sources, copies, sems):
    started = [
        pltpu.make_async_copy(source, copy, sems.at[n])
        for n, (source, copy) in enumerate(zip(sources, copies))
    ]
    for one in started:
        one.start()
    for one in started:
        one.wait()


def strips_kernel(x_in, cf_in, cc2_in, x, cf, cc2, row_out, col_out, corner_out, sems):
    fetch((x_in, cf_in, cc2_in), (x, cf, cc2), sems)
    rc, cc, feat = cf.shape
    r2, c2, _ = cc2.shape
    nr, nc, nk = RIM * cc, rc * RIM, RIM * RIM
    row_out[0:nr] = x[0:RIM].reshape(nr, feat)
    cols = x[:, 0:16, :].astype(F32)[:, :RIM]
    col_out[0:nc] = cols.reshape(nc, feat).astype(BF16)
    corner_out[0:nk] = cols[:RIM].reshape(nk, feat).astype(BF16)
    row_out[nr : 3 * nr] = cf[0 : 2 * RIM].reshape(2 * nr, feat)
    cols = cf[:, 0:16, :].astype(F32)[:, : 2 * RIM]
    col_out[nc : 3 * nc] = cols.reshape(2 * nc, feat).astype(BF16)
    corner_out[nk : 5 * nk] = cols[: 2 * RIM].reshape(4 * nk, feat).astype(BF16)
    cols = cc2[:, 0:16, :].astype(F32)[:, :RIM]
    for half in range(2):
        lanes = slice(half * feat, (half + 1) * feat)
        row_out[3 * nr + half * nr // 2 : 3 * nr + (half + 1) * nr // 2] = cc2[
            0:RIM, :, lanes
        ].reshape(nr // 2, feat)
        part = cols[:, :, lanes]
        col_out[3 * nc + half * nc // 2 : 3 * nc + (half + 1) * nc // 2] = part.reshape(
            nc // 2, feat
        ).astype(BF16)
        corner_out[5 * nk + half * nk : 5 * nk + (half + 1) * nk] = (
            part[:RIM].reshape(nk, feat).astype(BF16)
        )


def prepare_kernel(kept, *refs):
    sources, refs = refs[1 : 6 + kept], refs[6 + kept :]
    copies, refs, tables, near, sems = refs[:kept], refs[kept:-7], refs[-7], refs[-6:-1], refs[-1]
    fetch(sources, near + copies, sems)
    region1, region2, index, table1, table2 = near
    keys1, keys2, bias1, bias2, pairs_out = refs
    last = lax.axis_index(LAT) == lax.axis_size(LAT) - 1
    token = lax.broadcasted_iota(jnp.int32, (TOK, 128), 0)
    lane = lax.broadcasted_iota(jnp.int32, (TOK, 128), 1)
    for region, out in ((region1, keys1), (region2, keys2)):
        rows, columns = region.shape
        labels = jnp.broadcast_to(region[...][:, :, None], (rows, columns, 128))
        w = 0
        for a in range(rows // WIN):
            for b in range(columns // WIN):
                key = 2 * labels[WIN * a : WIN * (a + 1), WIN * b : WIN * (b + 1)].reshape(TOK, 128)
                if a == rows // WIN - 1:
                    key = key + jnp.where(
                        jnp.logical_and(last, token >= RIM * WIN), 1, 0
                    )
                onehot = jnp.where(key == lane, 1.0, 0.0).astype(BF16)
                out[w * TOK : (w + 1) * TOK, :] = same_keys(onehot)
                w += 1
    tables[...] = jnp.zeros(tables.shape, F32)
    h1, entries = table1.shape
    h2 = table2.shape[0]
    tables[0:h1, 0:entries] = table1[...]
    tables[8 : 8 + h2, 0:entries] = table2[...]
    turned = index[...].T
    at = jnp.concatenate([turned, turned], 1)
    pairs_out[...] = jnp.concatenate([turned[: TOK // 2], turned[TOK // 2 :]], 1)
    small = jnp.bitwise_and(at, 127)

    def looked_up(h):
        found = [
            jnp.take_along_axis(
                jnp.broadcast_to(tables[h : h + 1, p * 128 : (p + 1) * 128], (TOK, 128)), small, axis=1
            )
            for p in range(2)
        ]
        return jnp.where(at < 128, found[0], found[1])

    for out, base, heads in ((bias1, 0, h1), (bias2, 8, h2)):
        for p in range(heads // 2):
            out[:, p * 128 : (p + 1) * 128] = jnp.where(
                lane < 64, looked_up(base + 2 * p), looked_up(base + 2 * p + 1)
            )


def cores_kernel(keep, got, out):
    out[...] = (keep[...] + got[...]).reshape(out.shape).astype(BF16)


def sum_kernel(scale, parts, out):
    total = jnp.sum(parts[...].astype(F32), axis=0) * scale
    out[...] = jnp.broadcast_to(total[None], out.shape).astype(BF16)


def unpack_kernel(own, got, gain1, qkv1, out1, table1, mgain, merge, gain2, qkv2, out2, table2, field):
    other = other_core()
    field[1 - other] = own[...].astype(F32).reshape(HALF, 128)
    field[other] = got[...].astype(F32).reshape(HALF, 128)
    feat = out1.shape[0]
    feat2 = out2.shape[0]
    for b in range(6):
        qkv2[:, b * feat : (b + 1) * feat] = field[0, b * feat2 : (b + 1) * feat2, :]
    for b in range(2):
        out2[:, b * feat : (b + 1) * feat] = field[1, b * feat2 : (b + 1) * feat2, :]
        r0 = 2 * feat2 + b * 4 * feat
        merge[:, b * feat : (b + 1) * feat] = field[1, r0 : r0 + 4 * feat, :]
    for b in range(3):
        r0 = COARSE + b * feat
        qkv1[:, b * feat : (b + 1) * feat] = field[0, r0 : r0 + feat, :]
    out1[...] = field[1, COARSE : COARSE + feat, :]
    r0 = COARSE + feat
    tables = jnp.concatenate([field[1, r0 : r0 + 16, :], field[1, r0 + 16 : r0 + 32, :]], 1)
    h1, entries = table1.shape
    h2 = table2.shape[0]
    table1[...] = tables[0:h1, 0:entries]
    table2[...] = tables[h1 : h1 + h2, 0:entries]
    gains = field[1, r0 + 32 : r0 + 40, :]
    gain1[...] = gains[0:1]
    for q in range(4):
        mgain[:, q * feat : (q + 1) * feat] = gains[1 + q : 2 + q]
    for q in range(2):
        gain2[:, q * feat : (q + 1) * feat] = gains[5 + q : 6 + q]


def fine_forward_kernel(
    x, xr, xc, xk, keys, bias, gain, wqkv, wout,
    xw_out, qkv_out, mixed_out, own_out, row_out, col_out, corner_out,
    field, grid,
):
    rc, cc, feat = x.shape
    pulled(
        field, x[...], xr[: RIM * cc], xc[: rc * RIM], xk[: RIM * RIM], RIM, rc, cc
    )
    hm = head_masks()
    wide = cc // WIN
    group = 4
    for a in range(rc // WIN):
        for b0 in range(0, wide, group):
            r0 = RIM + WIN * a
            parts = [
                field[r0 : r0 + WIN, RIM + WIN * b : RIM + WIN * (b + 1), :].reshape(TOK, feat)
                for b in range(b0, b0 + group)
            ]
            tokens = jnp.concatenate(parts, 0)
            t0 = (a * wide + b0) * TOK
            span = pl.ds(t0, group * TOK)
            xw_out[span, :] = tokens.astype(BF16)
            hat, _ = unit_norm(tokens)
            normed = (hat * gain[...]).astype(BF16)
            qkv = nn_dot(normed, wqkv[...]).astype(BF16)
            qkv_out[span, :] = qkv
            mixed = []
            for n in range(group):
                w = a * wide + b0 + n
                rows = slice(n * TOK, (n + 1) * TOK)
                mixed.append(
                    unit_forward(
                        qkv[rows, :feat],
                        qkv[rows, feat : 2 * feat],
                        qkv[rows, 2 * feat :],
                        bias[...],
                        keys[w * TOK : (w + 1) * TOK, :],
                        hm,
                    )
                )
            mixed = jnp.concatenate(mixed, 0)
            mixed_out[span, :] = mixed
            result = tokens + nn_dot(mixed, wout[...])
            for n in range(group):
                b = b0 + n
                grid[WIN * a : WIN * (a + 1), WIN * b : WIN * (b + 1), :] = result[
                    n * TOK : (n + 1) * TOK
                ].reshape(WIN, WIN, feat)
    own_out[...] = grid[...].astype(BF16)
    row_out[...] = grid[0:RIM].reshape(RIM * cc, feat).astype(BF16)
    col_out[...] = grid[:, 0:RIM].reshape(rc * RIM, feat).astype(BF16)
    corner_out[...] = grid[0:RIM, 0:RIM].reshape(RIM * RIM, feat).astype(BF16)


def coarse_kernel(
    f, fr, fc, fk, cf, cc2, cr, ccl, ck,
    keys, bias, mgain, wmerge, gain, wqkv, wout,
    own_out, fine_out, row_out, col_out, corner_out,
    packed, gmgain, ggain, gbias,
    field, cfield, coarse_field, fgrid, cgrid,
):
    rc, cc, feat = f.shape
    r2, c2 = rc // 2, cc // 2
    feat2 = 2 * feat
    wide = c2 // WIN
    windows = [(a, b) for a in range(r2 // WIN) for b in range(wide)]
    count = len(windows) * TOK
    hm = head_masks()
    pulled(field, f[...], fr[...], fc[...], fk[...], RIM, rc, cc)
    nr, nc, nk = RIM * cc, rc * RIM, RIM * RIM
    pulled(cfield, cf[...], cr[nr : 3 * nr], ccl[nc : 3 * nc], ck[nk : 5 * nk], 2 * RIM, rc, cc)
    for half in range(2):
        lanes = slice(half * feat, (half + 1) * feat)
        pulled(
            coarse_field.at[half],
            cc2[:, :, lanes],
            cr[pl.ds(3 * nr + half * nr // 2, nr // 2)],
            ccl[pl.ds(3 * nc + half * nc // 2, nc // 2)],
            ck[pl.ds(5 * nk + half * nk, nk)],
            RIM,
            r2,
            c2,
        )

    def in_windows(load):
        return jnp.concatenate([load(a, b).reshape(TOK, feat) for a, b in windows], 0)

    def joined_part(ref, rim, quad):
        dc, dr = quad // 2, quad % 2

        def load(a, b):
            return jnp.stack(
                [
                    ref[
                        rim + 2 * (WIN * a + r) + dr,
                        pl.ds(rim + 2 * WIN * b + dc, WIN, stride=2),
                        :,
                    ]
                    for r in range(WIN)
                ],
                0,
            )

        return in_windows(load)

    parts = [joined_part(field, RIM, quad) for quad in range(4)]
    mean = sum(jnp.sum(p, axis=-1, keepdims=True) for p in parts) * (1.0 / (4 * feat))
    centered = [p - mean for p in parts]
    spread = sum(jnp.sum(p * p, axis=-1, keepdims=True) for p in centered) * (1.0 / (4 * feat))
    mrstd = lax.rsqrt(spread + EPSILON)
    mhat = [p * mrstd for p in centered]
    mgains = [mgain[:, q * feat : (q + 1) * feat] for q in range(4)]
    mnormed = jnp.concatenate([(h * g).astype(BF16) for h, g in zip(mhat, mgains)], 1)
    coarse_in = nn_dot(mnormed, wmerge[...]).astype(BF16).astype(F32)
    hat, rstd = unit_norm(coarse_in)
    normed = (hat * gain[...]).astype(BF16)
    qkv = nn_dot(normed, wqkv[...]).astype(BF16)
    mixed = []
    for w in range(len(windows)):
        rows = slice(w * TOK, (w + 1) * TOK)
        units = []
        same = keys[rows, :]
        for g in range(2):
            lo = g * feat
            units.append(
                unit_forward(
                    qkv[rows, lo : lo + feat],
                    qkv[rows, feat2 + lo : feat2 + lo + feat],
                    qkv[rows, 2 * feat2 + lo : 2 * feat2 + lo + feat],
                    bias[:, g * 4 * TOK : (g + 1) * 4 * TOK],
                    same,
                    hm,
                )
            )
        mixed.append(jnp.concatenate(units, 1))
    mixed = jnp.concatenate(mixed, 0)
    result = coarse_in + nn_dot(mixed, wout[...])
    for w, (a, b) in enumerate(windows):
        for half in range(2):
            cgrid[half, WIN * a : WIN * (a + 1), WIN * b : WIN * (b + 1), :] = result[
                w * TOK : (w + 1) * TOK, half * feat : (half + 1) * feat
            ].reshape(WIN, WIN, feat)
    cot = jnp.concatenate(
        [
            in_windows(
                lambda a, b: coarse_field[
                    half,
                    RIM + WIN * a : RIM + WIN * (a + 1),
                    RIM + WIN * b : RIM + WIN * (b + 1),
                    :,
                ]
            )
            for half in range(2)
        ],
        1,
    )
    cotb = cot.astype(BF16)
    grad = tn_dot(mixed, cotb)
    for b in range(2):
        packed[1, b * feat2 : (b + 1) * feat2, :] = grad[:, b * feat : (b + 1) * feat]
    cot_mixed = nt_dot(cotb, wout[...]).astype(BF16)
    cot_rows = []
    total = [jnp.zeros((TOK, 4 * TOK), F32) for _ in range(2)]
    for w in range(len(windows)):
        rows = slice(w * TOK, (w + 1) * TOK)
        dqs, dks, dvs = [], [], []
        same = keys[rows, :]
        for g in range(2):
            lo = g * feat
            dq, dk, dv, ds = unit_backward(
                qkv[rows, lo : lo + feat],
                qkv[rows, feat2 + lo : feat2 + lo + feat],
                qkv[rows, 2 * feat2 + lo : 2 * feat2 + lo + feat],
                cot_mixed[rows, lo : lo + feat],
                bias[:, g * 4 * TOK : (g + 1) * 4 * TOK],
                same,
                hm,
            )
            dqs.append(dq)
            dks.append(dk)
            dvs.append(dv)
            total[g] = total[g] + ds
        cot_rows.append(jnp.concatenate(dqs + dks + dvs, 1))
    gbias[...] = jnp.concatenate(total, 1)
    cot_qkv = jnp.concatenate(cot_rows, 0)
    grad = tn_dot(normed, cot_qkv)
    for b in range(6):
        packed[0, b * feat2 : (b + 1) * feat2, :] = grad[:, b * feat : (b + 1) * feat]
    cot_unit = nt_dot(cot_qkv, wqkv[...]).astype(BF16).astype(F32)
    ggain[...] = jnp.sum(cot_unit * hat, axis=0, keepdims=True)
    cot_in = (cot + norm_back(hat, rstd, cot_unit, gain[...])).astype(BF16)
    grad = tn_dot(mnormed, cot_in)
    for b in range(2):
        r0 = 2 * feat2 + b * 4 * feat
        packed[1, r0 : r0 + 4 * feat, :] = grad[:, b * feat : (b + 1) * feat]
    cot_norm = nt_dot(cot_in, wmerge[...]).astype(BF16).astype(F32)
    cot_parts = [cot_norm[:, q * feat : (q + 1) * feat] for q in range(4)]
    gmgain[...] = jnp.concatenate(
        [jnp.sum(c * h, axis=0, keepdims=True) for c, h in zip(cot_parts, mhat)], 1
    )
    ds = [c * g for c, g in zip(cot_parts, mgains)]
    mean_d = sum(jnp.sum(d, axis=-1, keepdims=True) for d in ds) * (1.0 / (4 * feat))
    mean_dh = sum(jnp.sum(d * h, axis=-1, keepdims=True) for d, h in zip(ds, mhat)) * (
        1.0 / (4 * feat)
    )
    for quad in range(4):
        dc, dr = quad // 2, quad % 2
        back = mrstd * (ds[quad] - mean_d - mhat[quad] * mean_dh)
        back = back + joined_part(cfield, 2 * RIM, quad)
        for w, (a, b) in enumerate(windows):
            for r in range(WIN):
                t0 = w * TOK + r * WIN
                fgrid[
                    2 * (WIN * a + r) + dr, pl.ds(2 * WIN * b + dc, WIN, stride=2), :
                ] = back[t0 : t0 + WIN]
    own_out[...] = cgrid[...].astype(BF16)
    fine_out[...] = fgrid[...].astype(BF16)
    row_out[...] = fgrid[rc - RIM :].reshape(nr, feat).astype(BF16)
    col_out[...] = fgrid[:, cc - RIM :].reshape(nc, feat).astype(BF16)
    corner_out[...] = fgrid[rc - RIM :, cc - RIM :].reshape(nk, feat).astype(BF16)


def fine_backward_kernel(
    c, d, er, ec, ek, xw, qkv_in, mixed_in, keys, bias, gain, wqkv, wout,
    gmgain, ggain2, gbias2, index, coarse_grads,
    own_out, row_out, col_out, corner_out, send_out, keep_out,
    field, grid, packed, spread,
):
    rc, cc, feat = c.shape
    r2, c2 = rc // 2, cc // 2
    nr, nc, nk = RIM * cc, rc * RIM, RIM * RIM
    pushed(field, c[...], er[...], ec[...], ek[...], RIM, rc, cc)
    hm = head_masks()
    wide = cc // WIN
    group = 4
    total = jnp.zeros((TOK, 4 * TOK), F32)
    total_gain = jnp.zeros((1, feat), F32)
    total_out = jnp.zeros((feat, feat), F32)
    total_qkv = jnp.zeros((feat, 3 * feat), F32)
    for a in range(rc // WIN):
        for b0 in range(0, wide, group):
            cot = jnp.concatenate(
                [
                    field[
                        WIN * a : WIN * (a + 1), WIN * b : WIN * (b + 1), :
                    ].reshape(TOK, feat)
                    for b in range(b0, b0 + group)
                ],
                0,
            )
            t0 = (a * wide + b0) * TOK
            span = pl.ds(t0, group * TOK)
            cotb = cot.astype(BF16)
            total_out = total_out + tn_dot(mixed_in[span, :], cotb)
            cot_mixed = nt_dot(cotb, wout[...]).astype(BF16)
            qkv = qkv_in[span, :]
            cot_rows = []
            for n in range(group):
                w = a * wide + b0 + n
                rows = slice(n * TOK, (n + 1) * TOK)
                dq, dk, dv, ds = unit_backward(
                    qkv[rows, :feat],
                    qkv[rows, feat : 2 * feat],
                    qkv[rows, 2 * feat :],
                    cot_mixed[rows],
                    bias[...],
                    keys[w * TOK : (w + 1) * TOK, :],
                    hm,
                )
                total = total + ds
                cot_rows.append(jnp.concatenate([dq, dk, dv], 1))
            cot_qkv = jnp.concatenate(cot_rows, 0)
            hat, rstd = unit_norm(xw[span, :].astype(F32))
            normed = (hat * gain[...]).astype(BF16)
            total_qkv = total_qkv + tn_dot(normed, cot_qkv)
            cot_unit = nt_dot(cot_qkv, wqkv[...]).astype(BF16).astype(F32)
            total_gain = total_gain + jnp.sum(cot_unit * hat, axis=0, keepdims=True)
            result = cot + norm_back(hat, rstd, cot_unit, gain[...])
            for n in range(group):
                b = b0 + n
                grid[WIN * a : WIN * (a + 1), WIN * b : WIN * (b + 1), :] = result[
                    n * TOK : (n + 1) * TOK
                ].reshape(WIN, WIN, feat)
    for b in range(3):
        packed[0, b * feat : (b + 1) * feat, :] = total_qkv[:, b * feat : (b + 1) * feat]
    packed[0, 3 * feat :, :] = jnp.zeros((feat, feat), F32)
    packed[1, 0:feat, :] = total_out
    tables = table_sums([total, gbias2[:, : 4 * TOK], gbias2[:, 4 * TOK :]], index, spread)
    packed[1, feat : feat + 16, :] = tables[:, :feat]
    packed[1, feat + 16 : feat + 32, :] = tables[:, feat:]
    gains = jnp.concatenate(
        [total_gain]
        + [gmgain[:, q * feat : (q + 1) * feat] for q in range(4)]
        + [ggain2[:, q * feat : (q + 1) * feat] for q in range(2)]
        + [jnp.zeros((1, feat), F32)],
        0,
    )
    packed[1, feat + 32 : feat + 40, :] = gains
    packed[1, feat + 40 :, :] = jnp.zeros((3 * feat - 40, feat), F32)
    other = other_core()
    send_out[0:COARSE, :] = coarse_grads[other]
    send_out[COARSE:HALF, :] = packed[other]
    keep_out[0:COARSE, :] = coarse_grads[1 - other]
    keep_out[COARSE:HALF, :] = packed[1 - other]
    own_out[...] = grid[...].astype(BF16)
    row_out[0:nr] = grid[rc - RIM :].reshape(nr, feat).astype(BF16)
    col_out[0:nc] = grid[:, cc - RIM :].reshape(nc, feat).astype(BF16)
    corner_out[0:nk] = grid[rc - RIM :, cc - RIM :].reshape(nk, feat).astype(BF16)
    coarse = d[...].astype(F32)
    for half in range(2):
        row_out[nr + half * nr // 2 : nr + (half + 1) * nr // 2] = (
            coarse[half, r2 - RIM :].reshape(nr // 2, feat).astype(BF16)
        )
        col_out[nc + half * nc // 2 : nc + (half + 1) * nc // 2] = (
            coarse[half, :, c2 - RIM :].reshape(nc // 2, feat).astype(BF16)
        )
        corner_out[nk + half * nk : nk + (half + 1) * nk] = (
            coarse[half, r2 - RIM :, c2 - RIM :].reshape(nk, feat).astype(BF16)
        )


def place_kernel(c, d, er, ec, ek, out, coarse_out, field, dfield):
    rc, cc, feat = c.shape
    r2, c2 = rc // 2, cc // 2
    nr, nc, nk = RIM * cc, rc * RIM, RIM * RIM
    pushed(field, c[...], er[0:nr], ec[0:nc], ek[0:nk], RIM, rc, cc)
    out[...] = field[0:rc, 0:cc].astype(BF16)
    for half in range(2):
        pushed(
            dfield.at[half],
            d[half],
            er[pl.ds(nr + half * nr // 2, nr // 2)],
            ec[pl.ds(nc + half * nc // 2, nc // 2)],
            ek[pl.ds(nk + half * nk, nk)],
            RIM,
            r2,
            c2,
        )
        coarse_out[:, :, half * feat : (half + 1) * feat] = dfield[half, 0:r2, 0:c2].astype(BF16)


def call(kernel, outs, scratch, *args):
    return pl.pallas_call(
        kernel,
        name=getattr(kernel, "func", kernel).__name__,
        out_shape=outs,
        scratch_shapes=[pltpu.VMEM(s, F32) for s in scratch],
        compiler_params=pltpu.CompilerParams(vmem_limit_bytes=VMEM_LIMIT),
    )(*args)


def sds(*shape, dtype=BF16):
    return jax.ShapeDtypeStruct(shape, dtype)


def send(rows, cols, corner, sense):
    nlat, nlon = lax.axis_size(LAT), lax.axis_size(LON)
    lat = [(i, (i + sense) % nlat) for i in range(nlat)]
    lon = [(i, (i + sense) % nlon) for i in range(nlon)]
    both = [
        (j * nlat + i, (j + sense) % nlon * nlat + (i + sense) % nlat)
        for i in range(nlat)
        for j in range(nlon)
    ]
    return (
        lax.ppermute(rows, LAT, lat),
        lax.ppermute(cols, LON, lon),
        lax.ppermute(corner, LON + LAT, both),
    )


def along_torus(values):
    return lax.all_to_all(values, CHIPS, 0, 0, tiled=False)


def per_device(
    tokens, region1, region2, bias_index, ln1_gain, qkv_weight1, out_weight1, bias_table1,
    merge_gain, merge_weight, ln2_gain, qkv_weight2, out_weight2, bias_table2, cot_fine, cot_coarse,
):
    rc, cc, feat = tokens.shape
    r2, c2, feat2 = cot_coarse.shape
    heads1, heads2 = bias_table1.shape[1], bias_table2.shape[1]
    entries = bias_table1.shape[0]
    n_tok = rc * cc
    nr, nc, nk = RIM * cc, rc * RIM, RIM * RIM
    f32 = partial(sds, dtype=F32)

    near = partial(pltpu.with_memory_space_constraint, memory_space=pltpu.HBM)
    far = pl.BlockSpec(memory_space=pltpu.HBM)
    params = pltpu.CompilerParams(vmem_limit_bytes=VMEM_LIMIT)
    fields = (tokens, cot_fine, cot_coarse)
    *fields, row, col, corner = pl.pallas_call(
        strips_kernel,
        out_shape=[sds(*v.shape) for v in fields]
        + [sds(4 * nr, feat), sds(4 * nc, feat), sds(7 * nk, feat)],
        in_specs=[far] * 3,
        scratch_shapes=[pltpu.SemaphoreType.DMA((3,))],
        compiler_params=params,
        name="strips",
    )(*[near(v) for v in fields])
    tokens, cot_fine, cot_coarse = fields
    small = (region1, region2, bias_index, bias_table1.T, bias_table2.T)
    kept = (
        ln1_gain.reshape(1, feat), ln2_gain.reshape(1, feat2), merge_gain.reshape(1, 4 * feat),
        qkv_weight1, out_weight1, merge_weight, qkv_weight2, out_weight2,
    )
    gain1, gain2, mgain, wqkv1, wout1, wmerge, wqkv2, wout2, keys1, keys2, bias1, bias2, pairs = pl.pallas_call(
        partial(prepare_kernel, len(kept)),
        out_shape=[sds(*v.shape, dtype=v.dtype) for v in kept]
        + [
            f32(n_tok, 128), f32(n_tok // 4, 128), f32(TOK, heads1 * TOK), f32(TOK, heads2 * TOK),
            sds(TOK // 2, 2 * TOK, dtype=jnp.int32),
        ],
        in_specs=[pl.BlockSpec(memory_space=pltpu.VMEM)] + [far] * (len(small) + len(kept)),
        scratch_shapes=[pltpu.VMEM((16, 256), F32)]
        + [pltpu.VMEM(v.shape, v.dtype) for v in small]
        + [pltpu.SemaphoreType.DMA((len(small) + len(kept),))],
        compiler_params=params,
        name="prepare",
    )(corner, *[near(v) for v in small + kept])
    row, col, corner = send(row, col, corner, -1)
    xw, qkv, mixed, fs, fr, fc, fk = call(
        fine_forward_kernel,
        (
            sds(n_tok, feat), sds(n_tok, 3 * feat), sds(n_tok, feat), sds(rc, cc, feat),
            sds(nr, feat), sds(nc, feat), sds(nk, feat),
        ),
        [(rc + RIM, cc + 2 * RIM, feat), (rc, cc, feat)],
        tokens, row, col, corner, keys1, bias1, gain1, wqkv1, wout1,
    )
    fr, fc, fk = send(fr, fc, fk, -1)
    cs, cfo, er, ec, ek, coarse_grads, gmgain, ggain2, gbias2 = call(
        coarse_kernel,
        (
            sds(2, r2, c2, feat), sds(rc, cc, feat), sds(nr, feat), sds(nc, feat), sds(nk, feat),
            f32(2, COARSE, feat), f32(1, 4 * feat), f32(1, feat2), f32(TOK, heads2 * TOK),
        ),
        [
            (rc + RIM, cc + 2 * RIM, feat), (rc + 2 * RIM, cc + 2 * RIM, feat),
            (2, r2 + RIM, c2 + 2 * RIM, feat), (rc, cc, feat), (2, r2, c2, feat),
        ],
        fs, fr, fc, fk, cot_fine, cot_coarse, row, col, corner,
        keys2, bias2, mgain, wmerge, gain2, wqkv2, wout2,
    )
    er, ec, ek = send(er, ec, ek, 1)
    back, br, bc, bk, sent, held = call(
        fine_backward_kernel,
        (
            sds(rc, cc, feat), sds(2 * nr, feat), sds(2 * nc, feat), sds(3 * nk, feat),
            f32(HALF, feat), f32(HALF, feat),
        ),
        [
            (rc + RIM, cc + 2 * RIM, feat), (rc, cc, feat), (2, HALF - COARSE, feat), (TOK // 2, 16, 128),
        ],
        cfo, cs, er, ec, ek, xw, qkv, mixed, keys1, bias1, gain1, wqkv1, wout1,
        gmgain, ggain2, gbias2, pairs, coarse_grads,
    )
    br, bc, bk = send(br, bc, bk, 1)
    got = lax.ppermute(sent, "c", [(0, 1), (1, 0)])
    chips = math.prod(lax.axis_size(a) for a in CHIPS)
    blocks = sds(chips, HALF // chips, feat)
    parts = along_torus(call(cores_kernel, blocks, [], held, got))
    scale = 4.0 / math.sqrt(n_tok * chips * lax.axis_size("c"))
    part = call(partial(sum_kernel, scale), blocks, [], parts)
    part, br, bc, bk = lax.optimization_barrier((part, br, bc, bk))
    part = along_torus(part)
    grad_tokens, coarse_out = call(
        place_kernel,
        (sds(rc, cc, feat), sds(r2, c2, feat2)),
        [(rc + RIM, cc + 2 * RIM, feat), (2, r2 + RIM, c2 + 2 * RIM, feat)],
        back, cs, br, bc, bk,
    )
    g = call(
        unpack_kernel,
        (
            f32(1, feat), f32(feat, 3 * feat), f32(feat, feat), f32(heads1, entries),
            f32(1, 4 * feat), f32(4 * feat, feat2), f32(1, feat2), f32(feat2, 3 * feat2),
            f32(feat2, feat2), f32(heads2, entries),
        ),
        [(2, HALF, feat)],
        part, lax.ppermute(part, "c", [(0, 1), (1, 0)]),
    )
    return (
        coarse_out, grad_tokens, g[0].reshape(-1), g[1], g[2], g[3].T, g[4].reshape(-1), g[5],
        g[6].reshape(-1), g[7], g[8], g[9].T,
    )


def solution(mesh):
    fine_mesh = jax.sharding.Mesh(
        mesh.devices.reshape(8, 2, 2, 4, 2), ("z", "yl", "yh", "x", "c")
    )
    grid = P(LAT, LON, None)
    flat = P(LAT, LON)
    return jax.shard_map(
        per_device,
        mesh=fine_mesh,
        in_specs=(grid, flat, flat) + (P(),) * 11 + (grid, grid),
        out_specs=(grid, grid) + (P(),) * 10,
        check_vma=False,
    )
```

```python
from functools import partial
import math

import jax
import jax.numpy as jnp
from jax import lax
from jax.experimental import pallas as pl
from jax.experimental.pallas import tpu as pltpu
from jax.sharding import PartitionSpec as P

WIN = 8
RIM = 4
TOK = WIN * WIN
EPSILON = 1e-05
MASKED = -1000000000.0
F32 = jnp.float32
BF16 = jnp.bfloat16
LON = ("z", "yl")
LAT = ("yh", "x", "c")
CHIPS = ("z", "yl", "yh", "x")
EXTRA_ROWS = 12
EXTRA_COLS = 16
LABELS = 16
VMEM_LIMIT = 24 * 1024 * 1024


def nt_dot(a, b):
    return lax.dot_general(a, b, (((1,), (1,)), ((), ())), preferred_element_type=F32)


def tn_dot(a, b):
    return lax.dot_general(a, b, (((0,), (0,)), ((), ())), preferred_element_type=F32)


def nn_dot(a, b):
    return jnp.dot(a, b, preferred_element_type=F32)


def head_masks():
    rows = lax.broadcasted_iota(jnp.int32, (4 * TOK, 128), 0) // TOK
    lanes = lax.broadcasted_iota(jnp.int32, (4 * TOK, 128), 1) // 32
    return rows == lanes


def spread_heads(pair, hm):
    return jnp.concatenate(
        [jnp.where(hm, jnp.concatenate([p] * 4, 0), jnp.zeros((), p.dtype)) for p in pair], 1
    )


def diagonal(pair):
    zero = jnp.zeros(pair[0].shape, pair[0].dtype)
    return jnp.concatenate(
        [jnp.concatenate([pair[0], zero], 1), jnp.concatenate([zero, pair[1]], 1)], 0
    )


def fold_heads(wide):
    head = lax.broadcasted_iota(jnp.int32, (TOK, 128), 1) // 32
    return jnp.where(
        head < 2,
        jnp.where(head < 1, wide[:TOK], wide[TOK : 2 * TOK]),
        jnp.where(head < 3, wide[2 * TOK : 3 * TOK], wide[3 * TOK :]),
    )


def by_query(weights, pair):
    turned = jnp.concatenate([weights[h] for h in range(4)], 1).T
    out = []
    for w in range(2):
        rows = jnp.concatenate(
            [turned[(2 * h + w) * TOK : (2 * h + w + 1) * TOK] for h in range(4)], 0
        )
        out.append(fold_heads(nn_dot(rows, pair[w])).astype(BF16))
    return out


def by_key(weights, spread):
    wide = nn_dot(weights.reshape(4 * TOK, 2 * TOK), spread)
    return [fold_heads(wide[:, w * 128 : (w + 1) * 128]).astype(BF16) for w in range(2)]


def probs(k4, q2, bias, same):
    scores = nt_dot(k4, q2).reshape(4, TOK, 2 * TOK) * (32 ** (-0.5)) + bias
    scores = jnp.where(same[None] > 0.5, scores, MASKED)
    top = jnp.max(scores, axis=1, keepdims=True)
    grown = jnp.exp(scores - top)
    return grown * (1.0 / jnp.sum(grown, axis=1, keepdims=True))


def unit_forward(q, k, v, bias, same, hm):
    weights = probs(spread_heads(k, hm), diagonal(q), bias, same).astype(BF16)
    return by_query(weights, v)


def unit_backward(q, k, v, g, bias, same, hm):
    q2, g2 = diagonal(q), diagonal(g)
    p = probs(spread_heads(k, hm), q2, bias, same)
    dp = nt_dot(spread_heads(v, hm), g2).astype(BF16).astype(F32).reshape(p.shape)
    ds = p * (dp - jnp.sum(p * dp, axis=1, keepdims=True))
    dsb = (ds * (32 ** (-0.5))).astype(BF16)
    return by_query(dsb, k), by_key(dsb, q2), by_key(p.astype(BF16), g2), ds


def same_keys(first, second):
    both = jnp.concatenate([first, second], 0)
    lane = lax.broadcasted_iota(jnp.int32, (TOK, 2 * TOK), 1)
    return jnp.where(lane < TOK, nt_dot(first, both), nt_dot(second, both))


def unit_norm(x):
    centered = x - jnp.mean(x, axis=-1, keepdims=True)
    rstd = lax.rsqrt(jnp.mean(centered * centered, axis=-1, keepdims=True) + EPSILON)
    return centered * rstd, rstd


def norm_back(hat, rstd, cot, gain):
    d = cot * gain
    return rstd * (
        d - jnp.mean(d, axis=-1, keepdims=True) - hat * jnp.mean(d * hat, axis=-1, keepdims=True)
    )


def pulled(field, own, rows, cols, corner, rim, rc, cc):
    feat = field.shape[-1]
    field[0:rc, 0:cc] = own.astype(F32)
    field[rc : rc + rim, 0:cc] = rows.astype(F32).reshape(rim, cc, feat)
    field[0:rc, cc : cc + rim] = cols.astype(F32).reshape(rc, rim, feat)
    field[rc : rc + rim, cc : cc + rim] = corner.astype(F32).reshape(rim, rim, feat)


def pushed(field, own, rows, cols, corner, rim, rc, cc):
    feat = field.shape[-1]
    field[rim : rim + rc, rim : rim + cc] = own.astype(F32)
    field[0:rim, rim : rim + cc] = rows.astype(F32).reshape(rim, cc, feat)
    field[rim : rim + rc, 0:rim] = cols.astype(F32).reshape(rc, rim, feat)
    field[0:rim, 0:rim] = corner.astype(F32).reshape(rim, rim, feat)


HALF = 2048
COARSE = 1536
SMALL = 40


def other_core():
    return 1 - lax.axis_index("c")


def table_sums(totals, index, spread):
    lane = lax.broadcasted_iota(jnp.int32, (TOK // 2, 128), 1)
    spread[...] = jnp.zeros(spread.shape, F32)
    head = 0
    for total in totals:
        for h in range(4):
            block = total[h] + pltpu.roll(total[h], TOK, 1)
            spread[:, head, :] = jnp.where(lane < TOK, block[: TOK // 2], block[TOK // 2 :])
            head += 1
    entry = lax.broadcasted_iota(jnp.int32, (256, 256), 0)
    sums = jnp.zeros((32, 256), F32)
    for q in range(TOK // 4):
        part = jnp.concatenate([spread[2 * q], spread[2 * q + 1]], 1)
        high = part.astype(BF16)
        low = (part - high.astype(F32)).astype(BF16)
        at = jnp.concatenate([index[2 * q : 2 * q + 1, :], index[2 * q + 1 : 2 * q + 2, :]], 1)
        chosen = jnp.where(entry == at, 1.0, 0.0).astype(BF16)
        sums = sums + nt_dot(jnp.concatenate([high, low], 0), chosen)
    return sums[:16] + sums[16:]


def fetch(sources, copies, sems):
    started = [
        pltpu.make_async_copy(source, copy, sems.at[n])
        for n, (source, copy) in enumerate(zip(sources, copies))
    ]
    for one in started:
        one.start()
    for one in started:
        one.wait()


def strip_sizes(rc, cc):
    nr, nc, nk = RIM * cc, rc * RIM, RIM * RIM
    row = EXTRA_ROWS * cc, 2 * nr, nr, LABELS
    col = rc * EXTRA_COLS, 2 * nc, nc, LABELS
    corner = EXTRA_ROWS * EXTRA_COLS, 4 * nk, 2 * nk, LABELS
    return [[sum(sizes[: n + 1]) for n in range(4)] for sizes in (row, col, corner)]


def strips_kernel(x_in, cf_in, cc2_in, region_in, x, cf, cc2, row_out, col_out, corner_out, region, labels, sems):
    fetch((x_in, cf_in, cc2_in, region_in), (x, cf, cc2, region), sems)
    rc, cc, feat = cf.shape
    r2, c2, _ = cc2.shape
    nr, nc, nk = RIM * cc, rc * RIM, RIM * RIM
    row, col, corner = strip_sizes(rc, cc)
    row_out[0 : row[0]] = x[0:EXTRA_ROWS].reshape(row[0], feat)
    cols = x[:, 0:EXTRA_COLS, :]
    col_out[0 : col[0]] = cols.reshape(col[0], feat)
    corner_out[0 : corner[0]] = cols[:EXTRA_ROWS].reshape(corner[0], feat)
    row_out[row[0] : row[1]] = cf[0 : 2 * RIM].reshape(2 * nr, feat)
    cols = cf[:, 0:16, :].astype(F32)[:, : 2 * RIM]
    col_out[col[0] : col[1]] = cols.reshape(2 * nc, feat).astype(BF16)
    corner_out[corner[0] : corner[1]] = cols[: 2 * RIM].reshape(4 * nk, feat).astype(BF16)
    cols = cc2[:, 0:16, :].astype(F32)[:, :RIM]
    for half in range(2):
        lanes = slice(half * feat, (half + 1) * feat)
        r0, c0, k0 = row[1] + half * nr // 2, col[1] + half * nc // 2, corner[1] + half * nk
        row_out[r0 : r0 + nr // 2] = cc2[0:RIM, :, lanes].reshape(nr // 2, feat)
        part = cols[:, :, lanes]
        col_out[c0 : c0 + nc // 2] = part.reshape(nc // 2, feat).astype(BF16)
        corner_out[k0 : k0 + nk] = part[:RIM].reshape(nk, feat).astype(BF16)
    labels[...] = jnp.zeros(labels.shape, F32)
    labels[0:rc, 0:cc] = region[...].astype(F32)
    for out, ends in ((row_out, row), (col_out, col), (corner_out, corner)):
        out[ends[2] : ends[3]] = labels[...].astype(BF16)


def prepare_kernel(kept, *refs):
    sources, refs = refs[1 : 6 + kept], refs[6 + kept :]
    copies, refs, tables, near, sems = refs[:kept], refs[kept:-7], refs[-7], refs[-6:-1], refs[-1]
    fetch(sources, near + copies, sems)
    region1, region2, index, table1, table2 = near
    keys1, keys2, bias1, bias2, pairs_out = refs
    last = lax.axis_index(LAT) == lax.axis_size(LAT) - 1
    token = lax.broadcasted_iota(jnp.int32, (TOK, 128), 0)
    lane = lax.broadcasted_iota(jnp.int32, (TOK, 128), 1)
    for region, out in ((region1, keys1), (region2, keys2)):
        rows, columns = region.shape
        labels = jnp.broadcast_to(region[...][:, :, None], (rows, columns, 128))
        onehots = []
        for a in range(rows // WIN):
            for b in range(columns // WIN):
                key = 2 * labels[WIN * a : WIN * (a + 1), WIN * b : WIN * (b + 1)].reshape(TOK, 128)
                if a == rows // WIN - 1:
                    key = key + jnp.where(jnp.logical_and(last, token >= RIM * WIN), 1, 0)
                onehots.append(jnp.where(key == lane, 1.0, 0.0).astype(BF16))
        for p in range(len(onehots) // 2):
            out[p * TOK : (p + 1) * TOK, :] = same_keys(onehots[2 * p], onehots[2 * p + 1])
    tables[...] = jnp.zeros(tables.shape, F32)
    h1, entries = table1.shape
    h2 = table2.shape[0]
    tables[0:h1, 0:entries] = table1[...]
    tables[8 : 8 + h2, 0:entries] = table2[...]
    turned = index[...].T
    at = jnp.concatenate([turned, turned], 1)
    pairs_out[...] = jnp.concatenate([turned[: TOK // 2], turned[TOK // 2 :]], 1)
    small = jnp.bitwise_and(at, 127)

    def looked_up(h):
        found = [
            jnp.take_along_axis(
                jnp.broadcast_to(tables[h : h + 1, p * 128 : (p + 1) * 128], (TOK, 128)), small, axis=1
            )
            for p in range(2)
        ]
        return jnp.where(at < 128, found[0], found[1])

    for out, base, heads in ((bias1, 0, h1), (bias2, 8, h2)):
        for h in range(heads):
            out[h] = looked_up(base + h)


def cores_kernel(keep, got, out):
    total = keep[...] + got[...]
    small = total[HALF - 128 : HALF - 128 + SMALL]
    rest = small - small.astype(BF16).astype(F32)
    total = jnp.concatenate(
        [total[: HALF - 128], small, rest, jnp.zeros((128 - 2 * SMALL, 128), F32)], 0
    )
    out[...] = total.reshape(out.shape).astype(BF16)


def sum_kernel(scale, parts, out):
    total = jnp.sum(parts[...].astype(F32), axis=0) * scale
    out[...] = jnp.broadcast_to(total[None], out.shape).astype(BF16)


def unpack_kernel(own, got, gain1, qkv1, out1, table1, mgain, merge, gain2, qkv2, out2, table2, field):
    other = other_core()
    field[1 - other] = own[...].astype(F32).reshape(HALF, 128)
    field[other] = got[...].astype(F32).reshape(HALF, 128)
    feat = out1.shape[0]
    feat2 = out2.shape[0]
    for b in range(6):
        qkv2[:, b * feat : (b + 1) * feat] = field[0, b * feat2 : (b + 1) * feat2, :]
    for b in range(2):
        out2[:, b * feat : (b + 1) * feat] = field[1, b * feat2 : (b + 1) * feat2, :]
        r0 = 2 * feat2 + b * 4 * feat
        merge[:, b * feat : (b + 1) * feat] = field[1, r0 : r0 + 4 * feat, :]
    for b in range(3):
        r0 = COARSE + b * feat
        qkv1[:, b * feat : (b + 1) * feat] = field[0, r0 : r0 + feat, :]
    out1[...] = field[1, COARSE : COARSE + feat, :]
    r0 = HALF - 128
    small = field[1, r0 : r0 + SMALL, :] + field[1, r0 + SMALL : r0 + 2 * SMALL, :]
    tables = jnp.concatenate([small[0:16], small[16:32]], 1)
    h1, entries = table1.shape
    h2 = table2.shape[0]
    table1[...] = tables[0:h1, 0:entries]
    table2[...] = tables[h1 : h1 + h2, 0:entries]
    gains = small[32:SMALL]
    gain1[...] = gains[0:1]
    for q in range(4):
        mgain[:, q * feat : (q + 1) * feat] = gains[1 + q : 2 + q]
    for q in range(2):
        gain2[:, q * feat : (q + 1) * feat] = gains[5 + q : 6 + q]


def fine_forward_kernel(
    x, xr, xc, xk, keys, bias, gain, wqkv, wout,
    xw_out, qkv_out, mixed_out, out,
    field, grid,
):
    rc, cc, feat = x.shape
    rows, cols = rc // WIN, cc // WIN
    row, col, corner = strip_sizes(rc, cc)
    field[0:rc, 0:cc] = x[...].astype(F32)
    field[rc:, 0:cc] = xr[: row[0]].astype(F32).reshape(EXTRA_ROWS, cc, feat)
    field[0:rc, cc:] = xc[: col[0]].astype(F32).reshape(rc, EXTRA_COLS, feat)
    field[rc:, cc:] = xk[: corner[0]].astype(F32).reshape(EXTRA_ROWS, EXTRA_COLS, feat)
    hm = head_masks()
    token = lax.broadcasted_iota(jnp.int32, (TOK, 128), 0)
    lane = lax.broadcasted_iota(jnp.int32, (TOK, 128), 1).astype(F32)
    last = lax.axis_index(LAT) == lax.axis_size(LAT) - 1
    below = xr[row[2] : row[3]].astype(F32)[:WIN, :cc]
    beside = xc[col[2] : col[3]].astype(F32)[:rc, :WIN]
    across = xk[corner[2] : corner[3]].astype(F32)[:WIN, :WIN]
    below = jnp.broadcast_to(below[:, :, None], (WIN, cc, 128))
    beside = jnp.broadcast_to(beside[:, :, None], (rc, WIN, 128))
    across = jnp.broadcast_to(across[:, :, None], (WIN, WIN, 128))

    def onehot(a, b):
        if a < rows:
            key = 2.0 * beside[WIN * a : WIN * (a + 1)].reshape(TOK, 128)
            if a == rows - 1:
                key = key + jnp.where(jnp.logical_and(last, token >= RIM * WIN), 1.0, 0.0)
        elif b < cols:
            key = 2.0 * below[:, WIN * b : WIN * (b + 1)].reshape(TOK, 128)
        else:
            key = 2.0 * across.reshape(TOK, 128)
        return jnp.where(key == lane, 1.0, 0.0).astype(BF16)

    own = [(a, b) for a in range(rows) for b in range(cols)]
    more = [(a, cols) for a in range(rows)] + [(rows, b) for b in range(cols + 1)]
    more = more + more[-1:] * (len(more) % 2)
    group = 4
    for windows in (own, more):
        for n0 in range(0, len(windows), group):
            now = windows[n0 : n0 + group]
            tokens = jnp.concatenate(
                [
                    field[
                        RIM + WIN * a : RIM + WIN * (a + 1), RIM + WIN * b : RIM + WIN * (b + 1), :
                    ].reshape(TOK, feat)
                    for a, b in now
                ],
                0,
            )
            hat, _ = unit_norm(tokens)
            normed = (hat * gain[...]).astype(BF16)
            qkv = nn_dot(normed, wqkv[...]).astype(BF16)
            mixed = []
            for n in range(0, len(now), 2):
                parts = [
                    [qkv[m * TOK : (m + 1) * TOK, i * feat : (i + 1) * feat] for m in (n, n + 1)]
                    for i in range(3)
                ]
                if windows is own:
                    pair = (n0 + n) // 2
                    same = keys[pair * TOK : (pair + 1) * TOK, :]
                else:
                    same = same_keys(onehot(*now[n]), onehot(*now[n + 1]))
                mixed += unit_forward(*parts, bias[...], same, hm)
            mixed = jnp.concatenate(mixed, 0)
            if windows is own:
                span = pl.ds(n0 * TOK, group * TOK)
                xw_out[span, :] = tokens.astype(BF16)
                qkv_out[span, :] = qkv
                mixed_out[span, :] = mixed
            result = tokens + nn_dot(mixed, wout[...])
            for n, (a, b) in enumerate(now):
                grid[WIN * a : WIN * (a + 1), WIN * b : WIN * (b + 1), :] = result[
                    n * TOK : (n + 1) * TOK
                ].reshape(WIN, WIN, feat)
    out[...] = grid[RIM : RIM + rc, RIM : RIM + cc, :].astype(BF16)


def coarse_kernel(
    f, cf, cc2, cr, ccl, ck,
    keys, bias, mgain, wmerge, gain, wqkv, wout,
    own_out, fine_out, row_out, col_out, corner_out,
    packed, gmgain, ggain, gbias,
    field, cfield, coarse_field, fgrid, cgrid,
):
    rc, cc, feat = f.shape
    r2, c2 = rc // 2, cc // 2
    feat2 = 2 * feat
    wide = c2 // WIN
    windows = [(a, b) for a in range(r2 // WIN) for b in range(wide)]
    count = len(windows) * TOK
    hm = head_masks()
    field[...] = f[...].astype(F32)
    nr, nc, nk = RIM * cc, rc * RIM, RIM * RIM
    row, col, corner = strip_sizes(rc, cc)
    pulled(
        cfield,
        cf[...],
        cr[row[0] : row[1]],
        ccl[col[0] : col[1]],
        ck[corner[0] : corner[1]],
        2 * RIM,
        rc,
        cc,
    )
    for half in range(2):
        pulled(
            coarse_field.at[half],
            cc2[:, :, half * feat : (half + 1) * feat],
            cr[pl.ds(row[1] + half * nr // 2, nr // 2)],
            ccl[pl.ds(col[1] + half * nc // 2, nc // 2)],
            ck[pl.ds(corner[1] + half * nk, nk)],
            RIM,
            r2,
            c2,
        )

    def in_windows(load):
        return jnp.concatenate([load(a, b).reshape(TOK, feat) for a, b in windows], 0)

    def joined_part(ref, rim, quad):
        dc, dr = quad // 2, quad % 2

        def load(a, b):
            return jnp.stack(
                [
                    ref[
                        rim + 2 * (WIN * a + r) + dr,
                        pl.ds(rim + 2 * WIN * b + dc, WIN, stride=2),
                        :,
                    ]
                    for r in range(WIN)
                ],
                0,
            )

        return in_windows(load)

    parts = [joined_part(field, 0, quad) for quad in range(4)]
    mean = sum(jnp.sum(p, axis=-1, keepdims=True) for p in parts) * (1.0 / (4 * feat))
    centered = [p - mean for p in parts]
    spread = sum(jnp.sum(p * p, axis=-1, keepdims=True) for p in centered) * (1.0 / (4 * feat))
    mrstd = lax.rsqrt(spread + EPSILON)
    mhat = [p * mrstd for p in centered]
    mgains = [mgain[:, q * feat : (q + 1) * feat] for q in range(4)]
    mnormed = jnp.concatenate([(h * g).astype(BF16) for h, g in zip(mhat, mgains)], 1)
    coarse_in = nn_dot(mnormed, wmerge[...]).astype(BF16).astype(F32)
    hat, rstd = unit_norm(coarse_in)
    normed = (hat * gain[...]).astype(BF16)
    qkv = nn_dot(normed, wqkv[...]).astype(BF16)
    def parts_of(wide, w, i, g):
        lo = i * feat2 + g * feat
        return [wide[m * TOK : (m + 1) * TOK, lo : lo + feat] for m in (w, w + 1)]

    mixed = []
    for w in range(0, len(windows), 2):
        same = keys[w // 2 * TOK : (w // 2 + 1) * TOK, :]
        units = [
            unit_forward(
                *[parts_of(qkv, w, i, g) for i in range(3)], bias[4 * g : 4 * g + 4], same, hm
            )
            for g in range(2)
        ]
        mixed += [jnp.concatenate([units[0][m], units[1][m]], 1) for m in range(2)]
    mixed = jnp.concatenate(mixed, 0)
    result = coarse_in + nn_dot(mixed, wout[...])
    for w, (a, b) in enumerate(windows):
        for half in range(2):
            cgrid[half, WIN * a : WIN * (a + 1), WIN * b : WIN * (b + 1), :] = result[
                w * TOK : (w + 1) * TOK, half * feat : (half + 1) * feat
            ].reshape(WIN, WIN, feat)
    cot = jnp.concatenate(
        [
            in_windows(
                lambda a, b: coarse_field[
                    half,
                    RIM + WIN * a : RIM + WIN * (a + 1),
                    RIM + WIN * b : RIM + WIN * (b + 1),
                    :,
                ]
            )
            for half in range(2)
        ],
        1,
    )
    cotb = cot.astype(BF16)
    grad = tn_dot(mixed, cotb)
    for b in range(2):
        packed[1, b * feat2 : (b + 1) * feat2, :] = grad[:, b * feat : (b + 1) * feat]
    cot_mixed = nt_dot(cotb, wout[...]).astype(BF16)
    cot_rows = []
    total = [0.0, 0.0]
    for w in range(0, len(windows), 2):
        same = keys[w // 2 * TOK : (w // 2 + 1) * TOK, :]
        found = []
        for g in range(2):
            dq, dk, dv, ds = unit_backward(
                *[parts_of(qkv, w, i, g) for i in range(3)],
                parts_of(cot_mixed, w, 0, g),
                bias[4 * g : 4 * g + 4],
                same,
                hm,
            )
            found.append((dq, dk, dv))
            total[g] = total[g] + ds
        for m in range(2):
            cot_rows.append(
                jnp.concatenate([found[g][i][m] for i in range(3) for g in range(2)], 1)
            )
    for g in range(2):
        gbias[4 * g : 4 * g + 4] = total[g]
    cot_qkv = jnp.concatenate(cot_rows, 0)
    grad = tn_dot(normed, cot_qkv)
    for b in range(6):
        packed[0, b * feat2 : (b + 1) * feat2, :] = grad[:, b * feat : (b + 1) * feat]
    cot_unit = nt_dot(cot_qkv, wqkv[...]).astype(BF16).astype(F32)
    ggain[...] = jnp.sum(cot_unit * hat, axis=0, keepdims=True)
    cot_in = (cot + norm_back(hat, rstd, cot_unit, gain[...])).astype(BF16)
    grad = tn_dot(mnormed, cot_in)
    for b in range(2):
        r0 = 2 * feat2 + b * 4 * feat
        packed[1, r0 : r0 + 4 * feat, :] = grad[:, b * feat : (b + 1) * feat]
    cot_norm = nt_dot(cot_in, wmerge[...]).astype(BF16).astype(F32)
    cot_parts = [cot_norm[:, q * feat : (q + 1) * feat] for q in range(4)]
    gmgain[...] = jnp.concatenate(
        [jnp.sum(c * h, axis=0, keepdims=True) for c, h in zip(cot_parts, mhat)], 1
    )
    ds = [c * g for c, g in zip(cot_parts, mgains)]
    mean_d = sum(jnp.sum(d, axis=-1, keepdims=True) for d in ds) * (1.0 / (4 * feat))
    mean_dh = sum(jnp.sum(d * h, axis=-1, keepdims=True) for d, h in zip(ds, mhat)) * (
        1.0 / (4 * feat)
    )
    for quad in range(4):
        dc, dr = quad // 2, quad % 2
        back = mrstd * (ds[quad] - mean_d - mhat[quad] * mean_dh)
        back = back + joined_part(cfield, 2 * RIM, quad)
        for w, (a, b) in enumerate(windows):
            for r in range(WIN):
                t0 = w * TOK + r * WIN
                fgrid[
                    2 * (WIN * a + r) + dr, pl.ds(2 * WIN * b + dc, WIN, stride=2), :
                ] = back[t0 : t0 + WIN]
    own_out[...] = cgrid[...].astype(BF16)
    fine_out[...] = fgrid[...].astype(BF16)
    row_out[...] = fgrid[rc - RIM :].reshape(nr, feat).astype(BF16)
    col_out[...] = fgrid[:, cc - RIM :].reshape(nc, feat).astype(BF16)
    corner_out[...] = fgrid[rc - RIM :, cc - RIM :].reshape(nk, feat).astype(BF16)


def fine_backward_kernel(
    c, d, er, ec, ek, xw, qkv_in, mixed_in, keys, bias, gain, wqkv, wout,
    gmgain, ggain2, gbias2, index, coarse_grads,
    own_out, row_out, col_out, corner_out, send_out, keep_out,
    field, grid, packed, spread,
):
    rc, cc, feat = c.shape
    r2, c2 = rc // 2, cc // 2
    nr, nc, nk = RIM * cc, rc * RIM, RIM * RIM
    pushed(field, c[...], er[...], ec[...], ek[...], RIM, rc, cc)
    hm = head_masks()
    wide = cc // WIN
    group = 4
    total = jnp.zeros((4, TOK, 2 * TOK), F32)
    total_gain = jnp.zeros((1, feat), F32)
    total_out = jnp.zeros((feat, feat), F32)
    total_qkv = jnp.zeros((feat, 3 * feat), F32)
    for a in range(rc // WIN):
        for b0 in range(0, wide, group):
            cot = jnp.concatenate(
                [
                    field[
                        WIN * a : WIN * (a + 1), WIN * b : WIN * (b + 1), :
                    ].reshape(TOK, feat)
                    for b in range(b0, b0 + group)
                ],
                0,
            )
            t0 = (a * wide + b0) * TOK
            span = pl.ds(t0, group * TOK)
            cotb = cot.astype(BF16)
            total_out = total_out + tn_dot(mixed_in[span, :], cotb)
            cot_mixed = nt_dot(cotb, wout[...]).astype(BF16)
            qkv = qkv_in[span, :]
            cot_rows = []
            for n in range(0, group, 2):
                pair = (a * wide + b0 + n) // 2
                parts = [
                    [qkv[m * TOK : (m + 1) * TOK, i * feat : (i + 1) * feat] for m in (n, n + 1)]
                    for i in range(3)
                ]
                dq, dk, dv, ds = unit_backward(
                    *parts,
                    [cot_mixed[m * TOK : (m + 1) * TOK] for m in (n, n + 1)],
                    bias[...],
                    keys[pair * TOK : (pair + 1) * TOK, :],
                    hm,
                )
                total = total + ds
                cot_rows += [jnp.concatenate([dq[m], dk[m], dv[m]], 1) for m in range(2)]
            cot_qkv = jnp.concatenate(cot_rows, 0)
            hat, rstd = unit_norm(xw[span, :].astype(F32))
            normed = (hat * gain[...]).astype(BF16)
            total_qkv = total_qkv + tn_dot(normed, cot_qkv)
            cot_unit = nt_dot(cot_qkv, wqkv[...]).astype(BF16).astype(F32)
            total_gain = total_gain + jnp.sum(cot_unit * hat, axis=0, keepdims=True)
            result = cot + norm_back(hat, rstd, cot_unit, gain[...])
            for n in range(group):
                b = b0 + n
                grid[WIN * a : WIN * (a + 1), WIN * b : WIN * (b + 1), :] = result[
                    n * TOK : (n + 1) * TOK
                ].reshape(WIN, WIN, feat)
    for b in range(3):
        packed[0, b * feat : (b + 1) * feat, :] = total_qkv[:, b * feat : (b + 1) * feat]
    packed[0, 3 * feat :, :] = jnp.zeros((feat, feat), F32)
    packed[1, 0:feat, :] = total_out
    tables = table_sums([total, gbias2[0:4], gbias2[4:8]], index, spread)
    packed[1, feat : 3 * feat, :] = jnp.zeros((2 * feat, feat), F32)
    r0 = 3 * feat
    packed[1, r0 : r0 + 16, :] = tables[:, :feat]
    packed[1, r0 + 16 : r0 + 32, :] = tables[:, feat:]
    gains = jnp.concatenate(
        [total_gain]
        + [gmgain[:, q * feat : (q + 1) * feat] for q in range(4)]
        + [ggain2[:, q * feat : (q + 1) * feat] for q in range(2)]
        + [jnp.zeros((1, feat), F32)],
        0,
    )
    packed[1, r0 + 32 : r0 + SMALL, :] = gains
    packed[1, r0 + SMALL :, :] = jnp.zeros((feat - SMALL, feat), F32)
    other = other_core()
    send_out[0:COARSE, :] = coarse_grads[other]
    send_out[COARSE:HALF, :] = packed[other]
    keep_out[0:COARSE, :] = coarse_grads[1 - other]
    keep_out[COARSE:HALF, :] = packed[1 - other]
    own_out[...] = grid[...].astype(BF16)
    row_out[0:nr] = grid[rc - RIM :].reshape(nr, feat).astype(BF16)
    col_out[0:nc] = grid[:, cc - RIM :].reshape(nc, feat).astype(BF16)
    corner_out[0:nk] = grid[rc - RIM :, cc - RIM :].reshape(nk, feat).astype(BF16)
    coarse = d[...].astype(F32)
    for half in range(2):
        row_out[nr + half * nr // 2 : nr + (half + 1) * nr // 2] = (
            coarse[half, r2 - RIM :].reshape(nr // 2, feat).astype(BF16)
        )
        col_out[nc + half * nc // 2 : nc + (half + 1) * nc // 2] = (
            coarse[half, :, c2 - RIM :].reshape(nc // 2, feat).astype(BF16)
        )
        corner_out[nk + half * nk : nk + (half + 1) * nk] = (
            coarse[half, r2 - RIM :, c2 - RIM :].reshape(nk, feat).astype(BF16)
        )


def place_kernel(c, d, er, ec, ek, out, coarse_out, field, dfield):
    rc, cc, feat = c.shape
    r2, c2 = rc // 2, cc // 2
    nr, nc, nk = RIM * cc, rc * RIM, RIM * RIM
    pushed(field, c[...], er[0:nr], ec[0:nc], ek[0:nk], RIM, rc, cc)
    out[...] = field[0:rc, 0:cc].astype(BF16)
    for half in range(2):
        pushed(
            dfield.at[half],
            d[half],
            er[pl.ds(nr + half * nr // 2, nr // 2)],
            ec[pl.ds(nc + half * nc // 2, nc // 2)],
            ek[pl.ds(nk + half * nk, nk)],
            RIM,
            r2,
            c2,
        )
        coarse_out[:, :, half * feat : (half + 1) * feat] = dfield[half, 0:r2, 0:c2].astype(BF16)


def call(kernel, outs, scratch, *args):
    return pl.pallas_call(
        kernel,
        name=getattr(kernel, "func", kernel).__name__,
        out_shape=outs,
        scratch_shapes=[pltpu.VMEM(s, F32) for s in scratch],
        compiler_params=pltpu.CompilerParams(vmem_limit_bytes=VMEM_LIMIT),
    )(*args)


def sds(*shape, dtype=BF16):
    return jax.ShapeDtypeStruct(shape, dtype)


def send(rows, cols, corner, sense):
    nlat, nlon = lax.axis_size(LAT), lax.axis_size(LON)
    lat = [(i, (i + sense) % nlat) for i in range(nlat)]
    lon = [(i, (i + sense) % nlon) for i in range(nlon)]
    both = [
        (j * nlat + i, (j + sense) % nlon * nlat + (i + sense) % nlat)
        for i in range(nlat)
        for j in range(nlon)
    ]
    return (
        lax.ppermute(rows, LAT, lat),
        lax.ppermute(cols, LON, lon),
        lax.ppermute(corner, LON + LAT, both),
    )


def along_torus(values):
    return lax.all_to_all(values, CHIPS, 0, 0, tiled=False)


def per_device(
    tokens, region1, region2, bias_index, ln1_gain, qkv_weight1, out_weight1, bias_table1,
    merge_gain, merge_weight, ln2_gain, qkv_weight2, out_weight2, bias_table2, cot_fine, cot_coarse,
):
    rc, cc, feat = tokens.shape
    r2, c2, feat2 = cot_coarse.shape
    heads1, heads2 = bias_table1.shape[1], bias_table2.shape[1]
    entries = bias_table1.shape[0]
    n_tok = rc * cc
    nr, nc, nk = RIM * cc, rc * RIM, RIM * RIM
    f32 = partial(sds, dtype=F32)

    near = partial(pltpu.with_memory_space_constraint, memory_space=pltpu.HBM)
    far = pl.BlockSpec(memory_space=pltpu.HBM)
    params = pltpu.CompilerParams(vmem_limit_bytes=VMEM_LIMIT)
    fields = (tokens, cot_fine, cot_coarse)
    *fields, row, col, corner = pl.pallas_call(
        strips_kernel,
        out_shape=[sds(*v.shape) for v in fields]
        + [sds(ends[-1], feat) for ends in strip_sizes(rc, cc)],
        in_specs=[far] * 4,
        scratch_shapes=[
            pltpu.VMEM(region1.shape, region1.dtype),
            pltpu.VMEM((LABELS, 128), F32),
            pltpu.SemaphoreType.DMA((4,)),
        ],
        compiler_params=params,
        name="strips",
    )(*[near(v) for v in fields + (region1,)])
    tokens, cot_fine, cot_coarse = fields
    small = (region1, region2, bias_index, bias_table1.T, bias_table2.T)
    kept = (
        ln1_gain.reshape(1, feat), ln2_gain.reshape(1, feat2), merge_gain.reshape(1, 4 * feat),
        qkv_weight1, out_weight1, merge_weight, qkv_weight2, out_weight2,
    )
    gain1, gain2, mgain, wqkv1, wout1, wmerge, wqkv2, wout2, keys1, keys2, bias1, bias2, pairs = pl.pallas_call(
        partial(prepare_kernel, len(kept)),
        out_shape=[sds(*v.shape, dtype=v.dtype) for v in kept]
        + [
            f32(n_tok // 2, 128), f32(n_tok // 8, 128), f32(heads1, TOK, 128), f32(heads2, TOK, 128),
            sds(TOK // 2, 2 * TOK, dtype=jnp.int32),
        ],
        in_specs=[pl.BlockSpec(memory_space=pltpu.VMEM)] + [far] * (len(small) + len(kept)),
        scratch_shapes=[pltpu.VMEM((16, 256), F32)]
        + [pltpu.VMEM(v.shape, v.dtype) for v in small]
        + [pltpu.SemaphoreType.DMA((len(small) + len(kept),))],
        compiler_params=params,
        name="prepare",
    )(corner, *[near(v) for v in small + kept])
    row, col, corner = send(row, col, corner, -1)
    xw, qkv, mixed, fs = call(
        fine_forward_kernel,
        (sds(n_tok, feat), sds(n_tok, 3 * feat), sds(n_tok, feat), sds(rc, cc, feat)),
        [(rc + EXTRA_ROWS, cc + EXTRA_COLS, feat), (rc + WIN, cc + WIN, feat)],
        tokens, row, col, corner, keys1, bias1, gain1, wqkv1, wout1,
    )
    cs, cfo, er, ec, ek, coarse_grads, gmgain, ggain2, gbias2 = call(
        coarse_kernel,
        (
            sds(2, r2, c2, feat), sds(rc, cc, feat), sds(nr, feat), sds(nc, feat), sds(nk, feat),
            f32(2, COARSE, feat), f32(1, 4 * feat), f32(1, feat2), f32(heads2, TOK, 2 * TOK),
        ),
        [
            (rc, cc, feat), (rc + 2 * RIM, cc + 2 * RIM, feat),
            (2, r2 + RIM, c2 + 2 * RIM, feat), (rc, cc, feat), (2, r2, c2, feat),
        ],
        fs, cot_fine, cot_coarse, row, col, corner,
        keys2, bias2, mgain, wmerge, gain2, wqkv2, wout2,
    )
    er, ec, ek = send(er, ec, ek, 1)
    back, br, bc, bk, sent, held = call(
        fine_backward_kernel,
        (
            sds(rc, cc, feat), sds(2 * nr, feat), sds(2 * nc, feat), sds(3 * nk, feat),
            f32(HALF, feat), f32(HALF, feat),
        ),
        [
            (rc + RIM, cc + 2 * RIM, feat), (rc, cc, feat), (2, HALF - COARSE, feat), (TOK // 2, 16, 128),
        ],
        cfo, cs, er, ec, ek, xw, qkv, mixed, keys1, bias1, gain1, wqkv1, wout1,
        gmgain, ggain2, gbias2, pairs, coarse_grads,
    )
    br, bc, bk = send(br, bc, bk, 1)
    got = lax.ppermute(sent, "c", [(0, 1), (1, 0)])
    chips = math.prod(lax.axis_size(a) for a in CHIPS)
    blocks = sds(chips, HALF // chips, feat)
    parts = along_torus(call(cores_kernel, blocks, [], held, got))
    scale = 4.0 / math.sqrt(n_tok * chips * lax.axis_size("c"))
    part = call(partial(sum_kernel, scale), blocks, [], parts)
    part, br, bc, bk = lax.optimization_barrier((part, br, bc, bk))
    part = along_torus(part)
    grad_tokens, coarse_out = call(
        place_kernel,
        (sds(rc, cc, feat), sds(r2, c2, feat2)),
        [(rc + RIM, cc + 2 * RIM, feat), (2, r2 + RIM, c2 + 2 * RIM, feat)],
        back, cs, br, bc, bk,
    )
    g = call(
        unpack_kernel,
        (
            f32(1, feat), f32(feat, 3 * feat), f32(feat, feat), f32(heads1, entries),
            f32(1, 4 * feat), f32(4 * feat, feat2), f32(1, feat2), f32(feat2, 3 * feat2),
            f32(feat2, feat2), f32(heads2, entries),
        ),
        [(2, HALF, feat)],
        part, lax.ppermute(part, "c", [(0, 1), (1, 0)]),
    )
    return (
        coarse_out, grad_tokens, g[0].reshape(-1), g[1], g[2], g[3].T, g[4].reshape(-1), g[5],
        g[6].reshape(-1), g[7], g[8], g[9].T,
    )


def solution(mesh):
    fine_mesh = jax.sharding.Mesh(
        mesh.devices.reshape(8, 2, 2, 4, 2), ("z", "yl", "yh", "x", "c")
    )
    grid = P(LAT, LON, None)
    flat = P(LAT, LON)
    return jax.shard_map(
        per_device,
        mesh=fine_mesh,
        in_specs=(grid, flat, flat) + (P(),) * 11 + (grid, grid),
        out_specs=(grid, grid) + (P(),) * 10,
        check_vma=False,
    )
```

```python
from functools import partial
import math

import jax
import jax.numpy as jnp
from jax import lax
from jax.experimental import pallas as pl
from jax.experimental.pallas import tpu as pltpu
from jax.sharding import PartitionSpec as P

WIN = 8
RIM = 4
TOK = WIN * WIN
EPSILON = 1e-05
MASKED = -1000000000.0
F32 = jnp.float32
BF16 = jnp.bfloat16
LON = ("z", "yl")
LAT = ("yh", "x", "c")
CHIPS = ("z", "yl", "yh", "x")
EXTRA_ROWS = 12
EXTRA_COLS = 16
LABELS = 16
VMEM_LIMIT = 24 * 1024 * 1024


def nt_dot(a, b):
    return lax.dot_general(a, b, (((1,), (1,)), ((), ())), preferred_element_type=F32)


def tn_dot(a, b):
    return lax.dot_general(a, b, (((0,), (0,)), ((), ())), preferred_element_type=F32)


def nn_dot(a, b):
    return jnp.dot(a, b, preferred_element_type=F32)


def head_masks():
    rows = lax.broadcasted_iota(jnp.int32, (4 * TOK, 128), 0) // TOK
    lanes = lax.broadcasted_iota(jnp.int32, (4 * TOK, 128), 1) // 32
    return rows == lanes


def spread_heads(pair, hm):
    return jnp.concatenate(
        [jnp.where(hm, jnp.concatenate([p] * 4, 0), jnp.zeros((), p.dtype)) for p in pair], 1
    )


def diagonal(pair):
    zero = jnp.zeros(pair[0].shape, pair[0].dtype)
    return jnp.concatenate(
        [jnp.concatenate([pair[0], zero], 1), jnp.concatenate([zero, pair[1]], 1)], 0
    )


def fold_heads(wide):
    head = lax.broadcasted_iota(jnp.int32, (TOK, 128), 1) // 32
    return jnp.where(
        head < 2,
        jnp.where(head < 1, wide[:TOK], wide[TOK : 2 * TOK]),
        jnp.where(head < 3, wide[2 * TOK : 3 * TOK], wide[3 * TOK :]),
    )


def by_query(weights, pairs):
    turned = [jnp.concatenate([p[h] for h in range(4)], 1).T for p in weights]
    rows = [
        [
            jnp.concatenate(
                [t[(2 * h + w) * TOK : (2 * h + w + 1) * TOK] for h in range(4)], 0
            )
            for w in range(2)
        ]
        for t in turned
    ]
    wide = [[nn_dot(r[w], pair[w]) for w in range(2)] for r, pair in zip(rows, pairs)]
    return [[fold_heads(w).astype(BF16) for w in both] for both in wide]


def by_key(weights, spread):
    wide = nn_dot(weights.reshape(4 * TOK, 2 * TOK), spread)
    return [fold_heads(wide[:, w * 128 : (w + 1) * 128]).astype(BF16) for w in range(2)]


def probs(k4, q2, bias, same):
    scores = [nt_dot(k, q).reshape(4, TOK, 2 * TOK) for k, q in zip(k4, q2)]
    scores = [
        jnp.where(m[None] > 0.5, s * (32 ** (-0.5)) + b, MASKED)
        for s, b, m in zip(scores, bias, same)
    ]
    tops = [jnp.max(s, axis=1, keepdims=True) for s in scores]
    grown = [jnp.exp(s - top) for s, top in zip(scores, tops)]
    sums = [jnp.sum(e, axis=1, keepdims=True) for e in grown]
    return [e * (1.0 / total) for e, total in zip(grown, sums)]


def units_forward(units, hm):
    q, k, v, bias, same = zip(*units)
    ps = probs([spread_heads(p, hm) for p in k], [diagonal(p) for p in q], bias, same)
    return by_query([p.astype(BF16) for p in ps], v)


def units_backward(units, hm):
    q, k, v, g, bias, same = zip(*units)
    q2 = [diagonal(p) for p in q]
    g2 = [diagonal(p) for p in g]
    ps = probs([spread_heads(p, hm) for p in k], q2, bias, same)
    dps = [nt_dot(spread_heads(p, hm), d) for p, d in zip(v, g2)]
    dps = [dp.astype(BF16).astype(F32).reshape(p.shape) for dp, p in zip(dps, ps)]
    sums = [jnp.sum(p * dp, axis=1, keepdims=True) for p, dp in zip(ps, dps)]
    dss = [p * (dp - total) for p, dp, total in zip(ps, dps, sums)]
    dsb = [(ds * (32 ** (-0.5))).astype(BF16) for ds in dss]
    dks = [by_key(d, p) for d, p in zip(dsb, q2)]
    dvs = [by_key(p.astype(BF16), d) for p, d in zip(ps, g2)]
    return list(zip(by_query(dsb, k), dks, dvs, dss))


def same_keys(first, second):
    both = jnp.concatenate([first, second], 0)
    lane = lax.broadcasted_iota(jnp.int32, (TOK, 2 * TOK), 1)
    return jnp.where(lane < TOK, nt_dot(first, both), nt_dot(second, both))


def unit_norm(x):
    centered = x - jnp.mean(x, axis=-1, keepdims=True)
    rstd = lax.rsqrt(jnp.mean(centered * centered, axis=-1, keepdims=True) + EPSILON)
    return centered * rstd, rstd


def norm_back(hat, rstd, cot, gain):
    d = cot * gain
    return rstd * (
        d - jnp.mean(d, axis=-1, keepdims=True) - hat * jnp.mean(d * hat, axis=-1, keepdims=True)
    )


def pulled(field, own, rows, cols, corner, rim, rc, cc):
    feat = field.shape[-1]
    field[0:rc, 0:cc] = own.astype(F32)
    field[rc : rc + rim, 0:cc] = rows.astype(F32).reshape(rim, cc, feat)
    field[0:rc, cc : cc + rim] = cols.astype(F32).reshape(rc, rim, feat)
    field[rc : rc + rim, cc : cc + rim] = corner.astype(F32).reshape(rim, rim, feat)


def pushed(field, own, rows, cols, corner, rim, rc, cc):
    feat = field.shape[-1]
    field[rim : rim + rc, rim : rim + cc] = own.astype(F32)
    field[0:rim, rim : rim + cc] = rows.astype(F32).reshape(rim, cc, feat)
    field[rim : rim + rc, 0:rim] = cols.astype(F32).reshape(rc, rim, feat)
    field[0:rim, 0:rim] = corner.astype(F32).reshape(rim, rim, feat)


HALF = 2048
COARSE = 1536
SMALL = 40


def other_core():
    return 1 - lax.axis_index("c")


def table_sums(totals, index, spread):
    lane = lax.broadcasted_iota(jnp.int32, (TOK // 2, 128), 1)
    spread[...] = jnp.zeros(spread.shape, F32)
    head = 0
    for total in totals:
        for h in range(4):
            block = total[h] + pltpu.roll(total[h], TOK, 1)
            spread[:, head, :] = jnp.where(lane < TOK, block[: TOK // 2], block[TOK // 2 :])
            head += 1
    entry = lax.broadcasted_iota(jnp.int32, (256, 256), 0)
    sums = jnp.zeros((32, 256), F32)
    for q in range(TOK // 4):
        part = jnp.concatenate([spread[2 * q], spread[2 * q + 1]], 1)
        high = part.astype(BF16)
        low = (part - high.astype(F32)).astype(BF16)
        at = jnp.concatenate([index[2 * q : 2 * q + 1, :], index[2 * q + 1 : 2 * q + 2, :]], 1)
        chosen = jnp.where(entry == at, 1.0, 0.0).astype(BF16)
        sums = sums + nt_dot(jnp.concatenate([high, low], 0), chosen)
    return sums[:16] + sums[16:]


def fetch(sources, copies, sems):
    started = [
        pltpu.make_async_copy(source, copy, sems.at[n])
        for n, (source, copy) in enumerate(zip(sources, copies))
    ]
    for one in started:
        one.start()
    for one in started:
        one.wait()


def strip_sizes(rc, cc):
    nr, nc, nk = RIM * cc, rc * RIM, RIM * RIM
    row = EXTRA_ROWS * cc, 2 * nr, nr, LABELS
    col = rc * EXTRA_COLS, 2 * nc, nc, LABELS
    corner = EXTRA_ROWS * EXTRA_COLS, 4 * nk, 2 * nk, LABELS
    return [[sum(sizes[: n + 1]) for n in range(4)] for sizes in (row, col, corner)]


def strips_kernel(x_in, cf_in, cc2_in, region_in, x, cf, cc2, row_out, col_out, corner_out, region, labels, sems):
    fetch((x_in, cf_in, cc2_in, region_in), (x, cf, cc2, region), sems)
    rc, cc, feat = cf.shape
    r2, c2, _ = cc2.shape
    nr, nc, nk = RIM * cc, rc * RIM, RIM * RIM
    row, col, corner = strip_sizes(rc, cc)
    row_out[0 : row[0]] = x[0:EXTRA_ROWS].reshape(row[0], feat)
    cols = x[:, 0:EXTRA_COLS, :]
    col_out[0 : col[0]] = cols.reshape(col[0], feat)
    corner_out[0 : corner[0]] = cols[:EXTRA_ROWS].reshape(corner[0], feat)
    row_out[row[0] : row[1]] = cf[0 : 2 * RIM].reshape(2 * nr, feat)
    cols = cf[:, 0:16, :].astype(F32)[:, : 2 * RIM]
    col_out[col[0] : col[1]] = cols.reshape(2 * nc, feat).astype(BF16)
    corner_out[corner[0] : corner[1]] = cols[: 2 * RIM].reshape(4 * nk, feat).astype(BF16)
    cols = cc2[:, 0:16, :].astype(F32)[:, :RIM]
    for half in range(2):
        lanes = slice(half * feat, (half + 1) * feat)
        r0, c0, k0 = row[1] + half * nr // 2, col[1] + half * nc // 2, corner[1] + half * nk
        row_out[r0 : r0 + nr // 2] = cc2[0:RIM, :, lanes].reshape(nr // 2, feat)
        part = cols[:, :, lanes]
        col_out[c0 : c0 + nc // 2] = part.reshape(nc // 2, feat).astype(BF16)
        corner_out[k0 : k0 + nk] = part[:RIM].reshape(nk, feat).astype(BF16)
    labels[...] = jnp.zeros(labels.shape, F32)
    labels[0:rc, 0:cc] = region[...].astype(F32)
    for out, ends in ((row_out, row), (col_out, col), (corner_out, corner)):
        out[ends[2] : ends[3]] = labels[...].astype(BF16)


def prepare_kernel(kept, *refs):
    sources, refs = refs[1 : 6 + kept], refs[6 + kept :]
    copies, refs, tables, near, sems = refs[:kept], refs[kept:-7], refs[-7], refs[-6:-1], refs[-1]
    fetch(sources, near + copies, sems)
    region1, region2, index, table1, table2 = near
    keys1, keys2, bias1, bias2, pairs_out = refs
    last = lax.axis_index(LAT) == lax.axis_size(LAT) - 1
    token = lax.broadcasted_iota(jnp.int32, (TOK, 128), 0)
    lane = lax.broadcasted_iota(jnp.int32, (TOK, 128), 1)
    for region, out in ((region1, keys1), (region2, keys2)):
        rows, columns = region.shape
        labels = jnp.broadcast_to(region[...][:, :, None], (rows, columns, 128))
        onehots = []
        for a in range(rows // WIN):
            for b in range(columns // WIN):
                key = 2 * labels[WIN * a : WIN * (a + 1), WIN * b : WIN * (b + 1)].reshape(TOK, 128)
                if a == rows // WIN - 1:
                    key = key + jnp.where(jnp.logical_and(last, token >= RIM * WIN), 1, 0)
                onehots.append(jnp.where(key == lane, 1.0, 0.0).astype(BF16))
        for p in range(len(onehots) // 2):
            out[p * TOK : (p + 1) * TOK, :] = same_keys(onehots[2 * p], onehots[2 * p + 1])
    tables[...] = jnp.zeros(tables.shape, F32)
    h1, entries = table1.shape
    h2 = table2.shape[0]
    tables[0:h1, 0:entries] = table1[...]
    tables[8 : 8 + h2, 0:entries] = table2[...]
    turned = index[...].T
    at = jnp.concatenate([turned, turned], 1)
    pairs_out[...] = jnp.concatenate([turned[: TOK // 2], turned[TOK // 2 :]], 1)
    small = jnp.bitwise_and(at, 127)

    def looked_up(h):
        found = [
            jnp.take_along_axis(
                jnp.broadcast_to(tables[h : h + 1, p * 128 : (p + 1) * 128], (TOK, 128)), small, axis=1
            )
            for p in range(2)
        ]
        return jnp.where(at < 128, found[0], found[1])

    for out, base, heads in ((bias1, 0, h1), (bias2, 8, h2)):
        for h in range(heads):
            out[h] = looked_up(base + h)


def cores_kernel(keep, got, out):
    total = keep[...] + got[...]
    small = total[HALF - 128 : HALF - 128 + SMALL]
    rest = small - small.astype(BF16).astype(F32)
    total = jnp.concatenate(
        [total[: HALF - 128], small, rest, jnp.zeros((128 - 2 * SMALL, 128), F32)], 0
    )
    out[...] = total.reshape(out.shape).astype(BF16)


def sum_kernel(scale, parts, out):
    total = jnp.sum(parts[...].astype(F32), axis=0) * scale
    out[...] = jnp.broadcast_to(total[None], out.shape).astype(BF16)


def unpack_kernel(own, got, gain1, qkv1, out1, table1, mgain, merge, gain2, qkv2, out2, table2, field):
    other = other_core()
    field[1 - other] = own[...].astype(F32).reshape(HALF, 128)
    field[other] = got[...].astype(F32).reshape(HALF, 128)
    feat = out1.shape[0]
    feat2 = out2.shape[0]
    for b in range(6):
        qkv2[:, b * feat : (b + 1) * feat] = field[0, b * feat2 : (b + 1) * feat2, :]
    for b in range(2):
        out2[:, b * feat : (b + 1) * feat] = field[1, b * feat2 : (b + 1) * feat2, :]
        r0 = 2 * feat2 + b * 4 * feat
        merge[:, b * feat : (b + 1) * feat] = field[1, r0 : r0 + 4 * feat, :]
    for b in range(3):
        r0 = COARSE + b * feat
        qkv1[:, b * feat : (b + 1) * feat] = field[0, r0 : r0 + feat, :]
    out1[...] = field[1, COARSE : COARSE + feat, :]
    r0 = HALF - 128
    small = field[1, r0 : r0 + SMALL, :] + field[1, r0 + SMALL : r0 + 2 * SMALL, :]
    tables = jnp.concatenate([small[0:16], small[16:32]], 1)
    h1, entries = table1.shape
    h2 = table2.shape[0]
    table1[...] = tables[0:h1, 0:entries]
    table2[...] = tables[h1 : h1 + h2, 0:entries]
    gains = small[32:SMALL]
    gain1[...] = gains[0:1]
    for q in range(4):
        mgain[:, q * feat : (q + 1) * feat] = gains[1 + q : 2 + q]
    for q in range(2):
        gain2[:, q * feat : (q + 1) * feat] = gains[5 + q : 6 + q]


def fine_forward_kernel(
    x, xr, xc, xk, keys, bias, gain, wqkv, wout,
    xw_out, qkv_out, mixed_out, out,
    field, grid,
):
    rc, cc, feat = x.shape
    rows, cols = rc // WIN, cc // WIN
    row, col, corner = strip_sizes(rc, cc)
    field[0:rc, 0:cc] = x[...].astype(F32)
    field[rc:, 0:cc] = xr[: row[0]].astype(F32).reshape(EXTRA_ROWS, cc, feat)
    field[0:rc, cc:] = xc[: col[0]].astype(F32).reshape(rc, EXTRA_COLS, feat)
    field[rc:, cc:] = xk[: corner[0]].astype(F32).reshape(EXTRA_ROWS, EXTRA_COLS, feat)
    hm = head_masks()
    token = lax.broadcasted_iota(jnp.int32, (TOK, 128), 0)
    lane = lax.broadcasted_iota(jnp.int32, (TOK, 128), 1).astype(F32)
    last = lax.axis_index(LAT) == lax.axis_size(LAT) - 1
    below = xr[row[2] : row[3]].astype(F32)[:WIN, :cc]
    beside = xc[col[2] : col[3]].astype(F32)[:rc, :WIN]
    across = xk[corner[2] : corner[3]].astype(F32)[:WIN, :WIN]
    below = jnp.broadcast_to(below[:, :, None], (WIN, cc, 128))
    beside = jnp.broadcast_to(beside[:, :, None], (rc, WIN, 128))
    across = jnp.broadcast_to(across[:, :, None], (WIN, WIN, 128))

    def onehot(a, b):
        if a < rows:
            key = 2.0 * beside[WIN * a : WIN * (a + 1)].reshape(TOK, 128)
            if a == rows - 1:
                key = key + jnp.where(jnp.logical_and(last, token >= RIM * WIN), 1.0, 0.0)
        elif b < cols:
            key = 2.0 * below[:, WIN * b : WIN * (b + 1)].reshape(TOK, 128)
        else:
            key = 2.0 * across.reshape(TOK, 128)
        return jnp.where(key == lane, 1.0, 0.0).astype(BF16)

    own = [(a, b) for a in range(rows) for b in range(cols)]
    more = [(a, cols) for a in range(rows)] + [(rows, b) for b in range(cols + 1)]
    more = more + more[-1:] * (len(more) % 2)
    now = own + more
    tokens = jnp.concatenate(
        [
            field[
                RIM + WIN * a : RIM + WIN * (a + 1), RIM + WIN * b : RIM + WIN * (b + 1), :
            ].reshape(TOK, feat)
            for a, b in now
        ],
        0,
    )
    hat, _ = unit_norm(tokens)
    normed = (hat * gain[...]).astype(BF16)
    qkv = nn_dot(normed, wqkv[...]).astype(BF16)
    units = []
    for n in range(0, len(now), 2):
        parts = [
            [qkv[m * TOK : (m + 1) * TOK, i * feat : (i + 1) * feat] for m in (n, n + 1)]
            for i in range(3)
        ]
        if n < len(own):
            same = keys[n // 2 * TOK : (n // 2 + 1) * TOK, :]
        else:
            same = same_keys(onehot(*now[n]), onehot(*now[n + 1]))
        units.append((*parts, bias[...], same))
    mixed = sum(units_forward(units, hm), [])
    mixed = jnp.concatenate(mixed, 0)
    count = len(own) * TOK
    xw_out[...] = tokens[:count].astype(BF16)
    qkv_out[...] = qkv[:count]
    mixed_out[...] = mixed[:count]
    result = tokens + nn_dot(mixed, wout[...])
    for n, (a, b) in enumerate(now):
        grid[WIN * a : WIN * (a + 1), WIN * b : WIN * (b + 1), :] = result[
            n * TOK : (n + 1) * TOK
        ].reshape(WIN, WIN, feat)
    out[...] = grid[RIM : RIM + rc, RIM : RIM + cc, :].astype(BF16)


def coarse_kernel(
    f, cf, cc2, cr, ccl, ck,
    keys, bias, mgain, wmerge, gain, wqkv, wout,
    own_out, fine_out, row_out, col_out, corner_out,
    packed, gmgain, ggain, gbias,
    field, cfield, coarse_field, fgrid, cgrid,
):
    rc, cc, feat = f.shape
    r2, c2 = rc // 2, cc // 2
    feat2 = 2 * feat
    wide = c2 // WIN
    windows = [(a, b) for a in range(r2 // WIN) for b in range(wide)]
    count = len(windows) * TOK
    hm = head_masks()
    field[...] = f[...].astype(F32)
    nr, nc, nk = RIM * cc, rc * RIM, RIM * RIM
    row, col, corner = strip_sizes(rc, cc)
    pulled(
        cfield,
        cf[...],
        cr[row[0] : row[1]],
        ccl[col[0] : col[1]],
        ck[corner[0] : corner[1]],
        2 * RIM,
        rc,
        cc,
    )
    for half in range(2):
        pulled(
            coarse_field.at[half],
            cc2[:, :, half * feat : (half + 1) * feat],
            cr[pl.ds(row[1] + half * nr // 2, nr // 2)],
            ccl[pl.ds(col[1] + half * nc // 2, nc // 2)],
            ck[pl.ds(corner[1] + half * nk, nk)],
            RIM,
            r2,
            c2,
        )

    def in_windows(load):
        return jnp.concatenate([load(a, b).reshape(TOK, feat) for a, b in windows], 0)

    def joined_part(ref, rim, quad):
        dc, dr = quad // 2, quad % 2

        def load(a, b):
            return jnp.stack(
                [
                    ref[
                        rim + 2 * (WIN * a + r) + dr,
                        pl.ds(rim + 2 * WIN * b + dc, WIN, stride=2),
                        :,
                    ]
                    for r in range(WIN)
                ],
                0,
            )

        return in_windows(load)

    parts = [joined_part(field, 0, quad) for quad in range(4)]
    mean = sum(jnp.sum(p, axis=-1, keepdims=True) for p in parts) * (1.0 / (4 * feat))
    centered = [p - mean for p in parts]
    spread = sum(jnp.sum(p * p, axis=-1, keepdims=True) for p in centered) * (1.0 / (4 * feat))
    mrstd = lax.rsqrt(spread + EPSILON)
    mhat = [p * mrstd for p in centered]
    mgains = [mgain[:, q * feat : (q + 1) * feat] for q in range(4)]
    mnormed = jnp.concatenate([(h * g).astype(BF16) for h, g in zip(mhat, mgains)], 1)
    coarse_in = nn_dot(mnormed, wmerge[...]).astype(BF16).astype(F32)
    hat, rstd = unit_norm(coarse_in)
    normed = (hat * gain[...]).astype(BF16)
    qkv = nn_dot(normed, wqkv[...]).astype(BF16)
    def parts_of(wide, w, i, g):
        lo = i * feat2 + g * feat
        return [wide[m * TOK : (m + 1) * TOK, lo : lo + feat] for m in (w, w + 1)]

    pairs = [(w, g) for w in range(0, len(windows), 2) for g in range(2)]
    units = [
        (
            *[parts_of(qkv, w, i, g) for i in range(3)],
            bias[4 * g : 4 * g + 4],
            keys[w // 2 * TOK : (w // 2 + 1) * TOK, :],
        )
        for w, g in pairs
    ]
    found = dict(zip(pairs, units_forward(units, hm)))
    mixed = [
        jnp.concatenate([found[w, 0][m], found[w, 1][m]], 1)
        for w in range(0, len(windows), 2)
        for m in range(2)
    ]
    mixed = jnp.concatenate(mixed, 0)
    result = coarse_in + nn_dot(mixed, wout[...])
    for w, (a, b) in enumerate(windows):
        for half in range(2):
            cgrid[half, WIN * a : WIN * (a + 1), WIN * b : WIN * (b + 1), :] = result[
                w * TOK : (w + 1) * TOK, half * feat : (half + 1) * feat
            ].reshape(WIN, WIN, feat)
    cot = jnp.concatenate(
        [
            in_windows(
                lambda a, b: coarse_field[
                    half,
                    RIM + WIN * a : RIM + WIN * (a + 1),
                    RIM + WIN * b : RIM + WIN * (b + 1),
                    :,
                ]
            )
            for half in range(2)
        ],
        1,
    )
    cotb = cot.astype(BF16)
    grad = tn_dot(mixed, cotb)
    for b in range(2):
        packed[1, b * feat2 : (b + 1) * feat2, :] = grad[:, b * feat : (b + 1) * feat]
    cot_mixed = nt_dot(cotb, wout[...]).astype(BF16)
    cot_rows = []
    units = [
        (*unit[:3], parts_of(cot_mixed, w, 0, g), *unit[3:]) for (w, g), unit in zip(pairs, units)
    ]
    found = dict(zip(pairs, units_backward(units, hm)))
    total = [sum(found[w, g][3] for w in range(0, len(windows), 2)) for g in range(2)]
    for w in range(0, len(windows), 2):
        for m in range(2):
            cot_rows.append(
                jnp.concatenate([found[w, g][i][m] for i in range(3) for g in range(2)], 1)
            )
    for g in range(2):
        gbias[4 * g : 4 * g + 4] = total[g]
    cot_qkv = jnp.concatenate(cot_rows, 0)
    grad = tn_dot(normed, cot_qkv)
    for b in range(6):
        packed[0, b * feat2 : (b + 1) * feat2, :] = grad[:, b * feat : (b + 1) * feat]
    cot_unit = nt_dot(cot_qkv, wqkv[...]).astype(BF16).astype(F32)
    ggain[...] = jnp.sum(cot_unit * hat, axis=0, keepdims=True)
    cot_in = (cot + norm_back(hat, rstd, cot_unit, gain[...])).astype(BF16)
    grad = tn_dot(mnormed, cot_in)
    for b in range(2):
        r0 = 2 * feat2 + b * 4 * feat
        packed[1, r0 : r0 + 4 * feat, :] = grad[:, b * feat : (b + 1) * feat]
    cot_norm = nt_dot(cot_in, wmerge[...]).astype(BF16).astype(F32)
    cot_parts = [cot_norm[:, q * feat : (q + 1) * feat] for q in range(4)]
    gmgain[...] = jnp.concatenate(
        [jnp.sum(c * h, axis=0, keepdims=True) for c, h in zip(cot_parts, mhat)], 1
    )
    ds = [c * g for c, g in zip(cot_parts, mgains)]
    mean_d = sum(jnp.sum(d, axis=-1, keepdims=True) for d in ds) * (1.0 / (4 * feat))
    mean_dh = sum(jnp.sum(d * h, axis=-1, keepdims=True) for d, h in zip(ds, mhat)) * (
        1.0 / (4 * feat)
    )
    for quad in range(4):
        dc, dr = quad // 2, quad % 2
        back = mrstd * (ds[quad] - mean_d - mhat[quad] * mean_dh)
        back = back + joined_part(cfield, 2 * RIM, quad)
        for w, (a, b) in enumerate(windows):
            for r in range(WIN):
                t0 = w * TOK + r * WIN
                fgrid[
                    2 * (WIN * a + r) + dr, pl.ds(2 * WIN * b + dc, WIN, stride=2), :
                ] = back[t0 : t0 + WIN]
    own_out[...] = cgrid[...].astype(BF16)
    fine_out[...] = fgrid[...].astype(BF16)
    row_out[...] = fgrid[rc - RIM :].reshape(nr, feat).astype(BF16)
    col_out[...] = fgrid[:, cc - RIM :].reshape(nc, feat).astype(BF16)
    corner_out[...] = fgrid[rc - RIM :, cc - RIM :].reshape(nk, feat).astype(BF16)


def fine_backward_kernel(
    c, d, er, ec, ek, xw, qkv_in, mixed_in, keys, bias, gain, wqkv, wout,
    gmgain, ggain2, gbias2, index, coarse_grads,
    own_out, row_out, col_out, corner_out, send_out, keep_out,
    field, grid, packed, spread,
):
    rc, cc, feat = c.shape
    r2, c2 = rc // 2, cc // 2
    nr, nc, nk = RIM * cc, rc * RIM, RIM * RIM
    pushed(field, c[...], er[...], ec[...], ek[...], RIM, rc, cc)
    hm = head_masks()
    wide = cc // WIN
    group = 16
    total = jnp.zeros((4, TOK, 2 * TOK), F32)
    total_gain = jnp.zeros((1, feat), F32)
    total_out = jnp.zeros((feat, feat), F32)
    total_qkv = jnp.zeros((feat, 3 * feat), F32)
    windows = [(a, b) for a in range(rc // WIN) for b in range(wide)]
    for n0 in range(0, len(windows), group):
        now = windows[n0 : n0 + group]
        cot = jnp.concatenate(
            [
                field[
                    WIN * a : WIN * (a + 1), WIN * b : WIN * (b + 1), :
                ].reshape(TOK, feat)
                for a, b in now
            ],
            0,
        )
        t0 = n0 * TOK
        span = pl.ds(t0, group * TOK)
        cotb = cot.astype(BF16)
        total_out = total_out + tn_dot(mixed_in[span, :], cotb)
        cot_mixed = nt_dot(cotb, wout[...]).astype(BF16)
        qkv = qkv_in[span, :]
        cot_rows = []
        units = []
        for n in range(0, group, 2):
            pair = (n0 + n) // 2
            parts = [
                [qkv[m * TOK : (m + 1) * TOK, i * feat : (i + 1) * feat] for m in (n, n + 1)]
                for i in range(3)
            ]
            parts.append([cot_mixed[m * TOK : (m + 1) * TOK] for m in (n, n + 1)])
            units.append((*parts, bias[...], keys[pair * TOK : (pair + 1) * TOK, :]))
        for dq, dk, dv, ds in units_backward(units, hm):
            total = total + ds
            cot_rows += [jnp.concatenate([dq[m], dk[m], dv[m]], 1) for m in range(2)]
        cot_qkv = jnp.concatenate(cot_rows, 0)
        hat, rstd = unit_norm(xw[span, :].astype(F32))
        normed = (hat * gain[...]).astype(BF16)
        total_qkv = total_qkv + tn_dot(normed, cot_qkv)
        cot_unit = nt_dot(cot_qkv, wqkv[...]).astype(BF16).astype(F32)
        total_gain = total_gain + jnp.sum(cot_unit * hat, axis=0, keepdims=True)
        result = cot + norm_back(hat, rstd, cot_unit, gain[...])
        for n, (a, b) in enumerate(now):
            grid[WIN * a : WIN * (a + 1), WIN * b : WIN * (b + 1), :] = result[
                n * TOK : (n + 1) * TOK
            ].reshape(WIN, WIN, feat)
    for b in range(3):
        packed[0, b * feat : (b + 1) * feat, :] = total_qkv[:, b * feat : (b + 1) * feat]
    packed[0, 3 * feat :, :] = jnp.zeros((feat, feat), F32)
    packed[1, 0:feat, :] = total_out
    tables = table_sums([total, gbias2[0:4], gbias2[4:8]], index, spread)
    packed[1, feat : 3 * feat, :] = jnp.zeros((2 * feat, feat), F32)
    r0 = 3 * feat
    packed[1, r0 : r0 + 16, :] = tables[:, :feat]
    packed[1, r0 + 16 : r0 + 32, :] = tables[:, feat:]
    gains = jnp.concatenate(
        [total_gain]
        + [gmgain[:, q * feat : (q + 1) * feat] for q in range(4)]
        + [ggain2[:, q * feat : (q + 1) * feat] for q in range(2)]
        + [jnp.zeros((1, feat), F32)],
        0,
    )
    packed[1, r0 + 32 : r0 + SMALL, :] = gains
    packed[1, r0 + SMALL :, :] = jnp.zeros((feat - SMALL, feat), F32)
    other = other_core()
    send_out[0:COARSE, :] = coarse_grads[other]
    send_out[COARSE:HALF, :] = packed[other]
    keep_out[0:COARSE, :] = coarse_grads[1 - other]
    keep_out[COARSE:HALF, :] = packed[1 - other]
    own_out[...] = grid[...].astype(BF16)
    row_out[0:nr] = grid[rc - RIM :].reshape(nr, feat).astype(BF16)
    col_out[0:nc] = grid[:, cc - RIM :].reshape(nc, feat).astype(BF16)
    corner_out[0:nk] = grid[rc - RIM :, cc - RIM :].reshape(nk, feat).astype(BF16)
    coarse = d[...].astype(F32)
    for half in range(2):
        row_out[nr + half * nr // 2 : nr + (half + 1) * nr // 2] = (
            coarse[half, r2 - RIM :].reshape(nr // 2, feat).astype(BF16)
        )
        col_out[nc + half * nc // 2 : nc + (half + 1) * nc // 2] = (
            coarse[half, :, c2 - RIM :].reshape(nc // 2, feat).astype(BF16)
        )
        corner_out[nk + half * nk : nk + (half + 1) * nk] = (
            coarse[half, r2 - RIM :, c2 - RIM :].reshape(nk, feat).astype(BF16)
        )


def place_kernel(c, d, er, ec, ek, out, coarse_out, field, dfield):
    rc, cc, feat = c.shape
    r2, c2 = rc // 2, cc // 2
    nr, nc, nk = RIM * cc, rc * RIM, RIM * RIM
    pushed(field, c[...], er[0:nr], ec[0:nc], ek[0:nk], RIM, rc, cc)
    out[...] = field[0:rc, 0:cc].astype(BF16)
    for half in range(2):
        pushed(
            dfield.at[half],
            d[half],
            er[pl.ds(nr + half * nr // 2, nr // 2)],
            ec[pl.ds(nc + half * nc // 2, nc // 2)],
            ek[pl.ds(nk + half * nk, nk)],
            RIM,
            r2,
            c2,
        )
        coarse_out[:, :, half * feat : (half + 1) * feat] = dfield[half, 0:r2, 0:c2].astype(BF16)


def call(kernel, outs, scratch, *args):
    return pl.pallas_call(
        kernel,
        name=getattr(kernel, "func", kernel).__name__,
        out_shape=outs,
        scratch_shapes=[pltpu.VMEM(s, F32) for s in scratch],
        compiler_params=pltpu.CompilerParams(vmem_limit_bytes=VMEM_LIMIT),
    )(*args)


def sds(*shape, dtype=BF16):
    return jax.ShapeDtypeStruct(shape, dtype)


def send(rows, cols, corner, sense):
    nlat, nlon = lax.axis_size(LAT), lax.axis_size(LON)
    lat = [(i, (i + sense) % nlat) for i in range(nlat)]
    lon = [(i, (i + sense) % nlon) for i in range(nlon)]
    both = [
        (j * nlat + i, (j + sense) % nlon * nlat + (i + sense) % nlat)
        for i in range(nlat)
        for j in range(nlon)
    ]
    return (
        lax.ppermute(rows, LAT, lat),
        lax.ppermute(cols, LON, lon),
        lax.ppermute(corner, LON + LAT, both),
    )


def along_torus(values):
    return lax.all_to_all(values, CHIPS, 0, 0, tiled=False)


def per_device(
    tokens, region1, region2, bias_index, ln1_gain, qkv_weight1, out_weight1, bias_table1,
    merge_gain, merge_weight, ln2_gain, qkv_weight2, out_weight2, bias_table2, cot_fine, cot_coarse,
):
    rc, cc, feat = tokens.shape
    r2, c2, feat2 = cot_coarse.shape
    heads1, heads2 = bias_table1.shape[1], bias_table2.shape[1]
    entries = bias_table1.shape[0]
    n_tok = rc * cc
    nr, nc, nk = RIM * cc, rc * RIM, RIM * RIM
    f32 = partial(sds, dtype=F32)

    near = partial(pltpu.with_memory_space_constraint, memory_space=pltpu.HBM)
    far = pl.BlockSpec(memory_space=pltpu.HBM)
    params = pltpu.CompilerParams(vmem_limit_bytes=VMEM_LIMIT)
    fields = (tokens, cot_fine, cot_coarse)
    *fields, row, col, corner = pl.pallas_call(
        strips_kernel,
        out_shape=[sds(*v.shape) for v in fields]
        + [sds(ends[-1], feat) for ends in strip_sizes(rc, cc)],
        in_specs=[far] * 4,
        scratch_shapes=[
            pltpu.VMEM(region1.shape, region1.dtype),
            pltpu.VMEM((LABELS, 128), F32),
            pltpu.SemaphoreType.DMA((4,)),
        ],
        compiler_params=params,
        name="strips",
    )(*[near(v) for v in fields + (region1,)])
    tokens, cot_fine, cot_coarse = fields
    small = (region1, region2, bias_index, bias_table1.T, bias_table2.T)
    kept = (
        ln1_gain.reshape(1, feat), ln2_gain.reshape(1, feat2), merge_gain.reshape(1, 4 * feat),
        qkv_weight1, out_weight1, merge_weight, qkv_weight2, out_weight2,
    )
    gain1, gain2, mgain, wqkv1, wout1, wmerge, wqkv2, wout2, keys1, keys2, bias1, bias2, pairs = pl.pallas_call(
        partial(prepare_kernel, len(kept)),
        out_shape=[sds(*v.shape, dtype=v.dtype) for v in kept]
        + [
            f32(n_tok // 2, 128), f32(n_tok // 8, 128), f32(heads1, TOK, 128), f32(heads2, TOK, 128),
            sds(TOK // 2, 2 * TOK, dtype=jnp.int32),
        ],
        in_specs=[pl.BlockSpec(memory_space=pltpu.VMEM)] + [far] * (len(small) + len(kept)),
        scratch_shapes=[pltpu.VMEM((16, 256), F32)]
        + [pltpu.VMEM(v.shape, v.dtype) for v in small]
        + [pltpu.SemaphoreType.DMA((len(small) + len(kept),))],
        compiler_params=params,
        name="prepare",
    )(corner, *[near(v) for v in small + kept])
    row, col, corner = send(row, col, corner, -1)
    xw, qkv, mixed, fs = call(
        fine_forward_kernel,
        (sds(n_tok, feat), sds(n_tok, 3 * feat), sds(n_tok, feat), sds(rc, cc, feat)),
        [(rc + EXTRA_ROWS, cc + EXTRA_COLS, feat), (rc + WIN, cc + WIN, feat)],
        tokens, row, col, corner, keys1, bias1, gain1, wqkv1, wout1,
    )
    cs, cfo, er, ec, ek, coarse_grads, gmgain, ggain2, gbias2 = call(
        coarse_kernel,
        (
            sds(2, r2, c2, feat), sds(rc, cc, feat), sds(nr, feat), sds(nc, feat), sds(nk, feat),
            f32(2, COARSE, feat), f32(1, 4 * feat), f32(1, feat2), f32(heads2, TOK, 2 * TOK),
        ),
        [
            (rc, cc, feat), (rc + 2 * RIM, cc + 2 * RIM, feat),
            (2, r2 + RIM, c2 + 2 * RIM, feat), (rc, cc, feat), (2, r2, c2, feat),
        ],
        fs, cot_fine, cot_coarse, row, col, corner,
        keys2, bias2, mgain, wmerge, gain2, wqkv2, wout2,
    )
    er, ec, ek = send(er, ec, ek, 1)
    back, br, bc, bk, sent, held = call(
        fine_backward_kernel,
        (
            sds(rc, cc, feat), sds(2 * nr, feat), sds(2 * nc, feat), sds(3 * nk, feat),
            f32(HALF, feat), f32(HALF, feat),
        ),
        [
            (rc + RIM, cc + 2 * RIM, feat), (rc, cc, feat), (2, HALF - COARSE, feat), (TOK // 2, 16, 128),
        ],
        cfo, cs, er, ec, ek, xw, qkv, mixed, keys1, bias1, gain1, wqkv1, wout1,
        gmgain, ggain2, gbias2, pairs, coarse_grads,
    )
    br, bc, bk = send(br, bc, bk, 1)
    got = lax.ppermute(sent, "c", [(0, 1), (1, 0)])
    chips = math.prod(lax.axis_size(a) for a in CHIPS)
    blocks = sds(chips, HALF // chips, feat)
    parts = along_torus(call(cores_kernel, blocks, [], held, got))
    scale = 4.0 / math.sqrt(n_tok * chips * lax.axis_size("c"))
    part = call(partial(sum_kernel, scale), blocks, [], parts)
    part, br, bc, bk = lax.optimization_barrier((part, br, bc, bk))
    part = along_torus(part)
    grad_tokens, coarse_out = call(
        place_kernel,
        (sds(rc, cc, feat), sds(r2, c2, feat2)),
        [(rc + RIM, cc + 2 * RIM, feat), (2, r2 + RIM, c2 + 2 * RIM, feat)],
        back, cs, br, bc, bk,
    )
    g = call(
        unpack_kernel,
        (
            f32(1, feat), f32(feat, 3 * feat), f32(feat, feat), f32(heads1, entries),
            f32(1, 4 * feat), f32(4 * feat, feat2), f32(1, feat2), f32(feat2, 3 * feat2),
            f32(feat2, feat2), f32(heads2, entries),
        ),
        [(2, HALF, feat)],
        part, lax.ppermute(part, "c", [(0, 1), (1, 0)]),
    )
    return (
        coarse_out, grad_tokens, g[0].reshape(-1), g[1], g[2], g[3].T, g[4].reshape(-1), g[5],
        g[6].reshape(-1), g[7], g[8], g[9].T,
    )


def solution(mesh):
    fine_mesh = jax.sharding.Mesh(
        mesh.devices.reshape(8, 2, 2, 4, 2), ("z", "yl", "yh", "x", "c")
    )
    grid = P(LAT, LON, None)
    flat = P(LAT, LON)
    return jax.shard_map(
        per_device,
        mesh=fine_mesh,
        in_specs=(grid, flat, flat) + (P(),) * 11 + (grid, grid),
        out_specs=(grid, grid) + (P(),) * 10,
        check_vma=False,
    )
```
